32 devices in a mesh: dp: 8 (over y, x, core), head: 4 (over z).
Axes of the slice: x: 2, y: 2, z: 4, core: 2. Of those that a mesh axis runs over, the one named last changes fastest.
Arguments:
- tokens: bfloat16 [8192, 768], P('dp'), may hold values from -6 to 6
- memory: bfloat16 [16, 2048, 768], P(None, ('dp', 'head')), may hold values from -6 to 6
- cotangent: bfloat16 [8192, 768], P('dp'), may hold values from -6 to 6
- lengths: int32 [64], P('dp'), may hold values from 0 to 1024, as said below
- groups: int32 [64], P('dp'), may hold values from 0 to 2
- image_map: int32 [64], P('dp'), may hold values from 0 to 15, as said below
- entry_weights: float32 [6, 768, 768], P(None, 'dp', 'head'), may hold values from -0.21875 to 0.21875
- exit_weights: float32 [2, 768, 768], P(None, 'head', 'dp'), may hold values from -1 to 1
- expand_weights: float32 [2, 768, 2048], P(None, 'dp', 'head'), may hold values from -0.21875 to 0.21875
- contract_weights: float32 [2048, 768], P('head', 'dp'), may hold values from -0.125 to 0.125
- norm_gains: float32 [3, 768], P(None, 'dp'), may hold values from 0.4 to 2.4
- entry_first: float32 [6, 768, 768], P(None, 'dp', 'head'), may hold values from -112 to 112
- entry_second: float32 [6, 768, 768], P(None, 'dp', 'head'), may hold values from 24.576 to 98.304
- exit_first: float32 [2, 768, 768], P(None, 'head', 'dp'), may hold values from -14 to 14
- exit_second: float32 [2, 768, 768], P(None, 'head', 'dp'), may hold values from 0.385024 to 1.55648
- expand_first: float32 [2, 768, 2048], P(None, 'dp', 'head'), may hold values from -32 to 32
- expand_second: float32 [2, 768, 2048], P(None, 'dp', 'head'), may hold values from 2.21184 to 8.84736
- contract_first: float32 [2048, 768], P('head', 'dp'), may hold values from -40 to 40
- contract_second: float32 [2048, 768], P('head', 'dp'), may hold values from 4.42368 to 18.0224
- gains_first: float32 [3, 768], P(None, 'dp'), may hold values from -160 to 160
- gains_second: float32 [3, 768], P(None, 'dp'), may hold values from 55.296 to 221.184
Outputs:
- output: float32 [8192, 768], P('dp')
- token_grads: float32 [8192, 768], P('dp')
- memory_grads: float32 [16, 2048, 768], P(None, ('dp', 'head'))
- entry_grads: float32 [6, 768, 768], P(None, 'dp', 'head')
- exit_grads: float32 [2, 768, 768], P(None, 'head', 'dp')
- expand_grads: float32 [2, 768, 2048], P(None, 'dp', 'head')
- contract_grads: float32 [2048, 768], P('head', 'dp')
- gain_grads: float32 [3, 768], P(None, 'dp')
- entry_mean: float32 [6, 768, 768], P(None, 'dp', 'head')
- exit_mean: float32 [2, 768, 768], P(None, 'head', 'dp')
- expand_mean: float32 [2, 768, 2048], P(None, 'dp', 'head')
- contract_mean: float32 [2048, 768], P('head', 'dp')
- gains_mean: float32 [3, 768], P(None, 'dp')
- entry_square: float32 [6, 768, 768], P(None, 'dp', 'head')
- exit_square: float32 [2, 768, 768], P(None, 'head', 'dp')
- expand_square: float32 [2, 768, 2048], P(None, 'dp', 'head')
- contract_square: float32 [2048, 768], P('head', 'dp')
- gains_square: float32 [3, 768], P(None, 'dp')
- entry_new: float32 [6, 768, 768], P(None, 'dp', 'head')
- exit_new: float32 [2, 768, 768], P(None, 'head', 'dp')
- expand_new: float32 [2, 768, 2048], P(None, 'dp', 'head')
- contract_new: float32 [2048, 768], P('head', 'dp')
- gains_new: float32 [3, 768], P(None, 'dp')
- entry_copy: bfloat16 [6, 768, 768], P(None, 'dp', 'head')
- exit_copy: bfloat16 [2, 768, 768], P(None, 'head', 'dp')
- expand_copy: bfloat16 [2, 768, 2048], P(None, 'dp', 'head')
- contract_copy: bfloat16 [2048, 768], P('head', 'dp')
- trust_norms: float32 [2, 14], replicated
The draws below stay inside these ranges and needn't reach their ends.
Inputs may be any that keep to these rules, and one draw needn't show every extreme that they name: Each dp group's 8 lengths sum to at most 1024; entries may be 0; in every draw some group holds a single text of 1024 tokens. `image_map`: A text of dp group i reads one of images i * 2 to (i + 1) * 2 - 1, and each of these is read by exactly 4 texts of the group.
All inputs are finite; a program needn't handle non-finite values.
Results may differ from the reference program's by a relative error of at most 0.025.
The reference program's roundings to bfloat16 on the way count: a program that leaves them out, or rounds other values in their place, can miss the bound.
Values may be sent and summed in bfloat16 or wider, within the bound.
No kernel may reach another device: no remote copies, remote signals or barrier semaphores. Data moves between devices by JAX's collectives and lax.ppermute only.
A program may use at most 192 MiB of HBM per device.

```python
import math
import jax
import jax.numpy as jnp
from jax import lax

HEADS = 12
HEAD_DIM = 64
D = 768
FF = 2048
TOK_DEV = 1024
TEXT_DEV = 8
IMG_DEV = 2
PATCHES = 2048
STEPS_DONE = 10
TOKENS = 8192
TEXTS = 64
IMAGES = 16
N_DP = 8


def draw_lengths(key, part):
    key = jax.random.fold_in(key, 11)
    key_total, key_cuts, key_full = jax.random.split(key, 3)
    row_count = TEXTS // TEXT_DEV
    totals = jax.random.randint(key_total, (row_count, 1), TOK_DEV // 2, TOK_DEV + 1)
    raw_cuts = jnp.sort(jax.random.randint(key_cuts, (row_count, TEXT_DEV - 1), 0, TOK_DEV + 1), axis=1)
    cuts = raw_cuts * totals // TOK_DEV
    bounds = jnp.concatenate([jnp.zeros((row_count, 1), jnp.int32), cuts, totals], axis=1)
    pieces = bounds[:, 1:] - bounds[:, :-1]
    full_row = jax.random.randint(key_full, (), 0, row_count)
    whole_text = jnp.zeros((row_count, TEXT_DEV), jnp.int32).at[:, 0].set(TOK_DEV)
    chosen = (jnp.arange(row_count) == full_row)[:, None]
    return jnp.where(chosen, whole_text, pieces).reshape(-1).astype(jnp.int32)


def shuffled(row_key):
    return jax.random.permutation(row_key, TEXT_DEV)


def draw_image_map(key, part):
    key = jax.random.fold_in(key, 13)
    row_count = TEXTS // TEXT_DEV
    row_keys = jax.random.split(key, row_count)
    orders = jax.vmap(shuffled)(row_keys)
    return (jnp.arange(row_count, dtype=jnp.int32)[:, None] * IMG_DEV + orders % IMG_DEV).reshape(-1).astype(jnp.int32)


def draw_norm_gains(key, part):
    key = jax.random.fold_in(key, 17)
    ramp = 0.6 + 1.2 * jnp.arange(D, dtype=jnp.float32) / D
    noise = jax.random.uniform(key, (3, D), jnp.float32, 0.85, 1.15)
    return (ramp[None, :] * noise).astype(jnp.float32)


def place_ends(values, rng, low, largest):
    extent = values.shape
    place = [jax.random.randint(jax.random.fold_in(rng, axis), (), 0, extent[axis]) for axis in range(len(extent))]
    values = values.at[tuple(place)].set(low)
    longest = extent.index(max(extent))
    place[longest] = (place[longest] + 1) % extent[longest]
    return values.at[tuple(place)].set(largest)


def block_scale(key, extent, cuts, least, high):
    factor_of = 1.0
    for dim, blocks in cuts:
        steps = jax.random.uniform(jax.random.fold_in(jax.random.fold_in(key, 6), dim), (blocks,), jnp.float32, least / len(cuts), high / len(cuts))
        factor_of = factor_of * jnp.repeat(jnp.exp(steps), extent[dim] // blocks).reshape((-1,) + (1,) * (len(extent) - 1 - dim))
    return factor_of


def gaussian(own_key, dims, deviation, most, cuts=(), kind=jnp.bfloat16):
    drawn = jax.random.normal(own_key, dims, jnp.float32) * deviation
    if len(cuts) > 0:
        drawn = block_scale(own_key, dims, cuts, -0.22, 0.18) * drawn
    return jnp.clip(drawn, min=-most, max=most).astype(kind)


def setup_inputs(seed: int = 0) -> dict:
    streams_of = jax.random.split(jax.random.key(seed), 22)
    tokens = gaussian(streams_of[0], (TOKENS, D), 1.0, 6.0, ((0, 8),))
    memory = gaussian(streams_of[1], (IMAGES, PATCHES, D), 1.0, 6.0, ((1, 32),))
    cotangent = gaussian(streams_of[2], (TOKENS, D), 1.0, 6.0, ((0, 8),))
    lengths = draw_lengths(jax.random.fold_in(streams_of[21], 71), 0)
    groups = place_ends(jax.random.randint(streams_of[4], (TEXTS,), 0, 3), jax.random.fold_in(streams_of[4], 1), 0, 2).astype(jnp.int32)
    image_map = draw_image_map(jax.random.fold_in(streams_of[21], 71), 0)
    entry_weights = gaussian(streams_of[6], (6, D, D), D ** -0.5, 0.21875, ((1, 8), (2, 4)), jnp.float32)
    exit_weights = gaussian(streams_of[7], (2, D, D), 32 ** -0.5, 1.0, ((1, 4), (2, 8)), jnp.float32)
    expand_weights = gaussian(streams_of[8], (2, D, FF), D ** -0.5, 0.21875, ((1, 8), (2, 4)), jnp.float32)
    contract_weights = gaussian(streams_of[9], (FF, D), FF ** -0.5, 0.125, ((0, 4), (1, 8)), jnp.float32)
    norm_gains = draw_norm_gains(jax.random.fold_in(streams_of[21], 71), 0)
    entry_first = gaussian(streams_of[11], (6, D, D), (0.22 * (0.75 * TOKENS) ** 0.5), 112.0, ((1, 8), (2, 4)), jnp.float32)
    entry_second = jnp.clip(jnp.exp(math.log(98.304) - 1.3862944 * jax.random.uniform(streams_of[12], (6, D, D), jnp.float32) ** block_scale(streams_of[12], (6, D, D), ((1, 8), (2, 4)), -0.2, 0.2)), 24.576, 98.304)
    exit_first = gaussian(streams_of[13], (2, D, D), (0.0275 * (0.75 * TOKENS) ** 0.5), 14.0, ((1, 4), (2, 8)), jnp.float32)
    exit_second = jnp.clip(jnp.exp(math.log(1.55648) - 1.3968765 * jax.random.uniform(streams_of[14], (2, D, D), jnp.float32) ** block_scale(streams_of[14], (2, D, D), ((1, 4), (2, 8)), -0.2, 0.2)), 0.385024, 1.55648)
    expand_first = gaussian(streams_of[15], (2, D, FF), (0.066 * (0.75 * TOKENS) ** 0.5), 32.0, ((1, 8), (2, 4)), jnp.float32)
    expand_second = jnp.clip(jnp.exp(math.log(8.84736) - 1.3862944 * jax.random.uniform(streams_of[16], (2, D, FF), jnp.float32) ** block_scale(streams_of[16], (2, D, FF), ((1, 8), (2, 4)), -0.2, 0.2)), 2.21184, 8.84736)
    contract_first = gaussian(streams_of[17], (FF, D), (0.094 * (0.75 * TOKENS) ** 0.5), 40.0, ((0, 4), (1, 8)), jnp.float32)
    contract_second = jnp.clip(jnp.exp(math.log(18.0224) - 1.4046435 * jax.random.uniform(streams_of[18], (FF, D), jnp.float32) ** block_scale(streams_of[18], (FF, D), ((0, 4), (1, 8)), -0.2, 0.2)), 4.42368, 18.0224)
    gains_first = gaussian(streams_of[19], (3, D), (0.33 * (0.75 * TOKENS) ** 0.5), 160.0, ((1, 8),), jnp.float32)
    gains_second = jnp.clip(jnp.exp(math.log(221.184) - 1.3862944 * jax.random.uniform(streams_of[20], (3, D), jnp.float32) ** block_scale(streams_of[20], (3, D), ((1, 8),), -0.2, 0.2)), 55.296, 221.184)
    return {"tokens": tokens, "memory": memory, "cotangent": cotangent, "lengths": lengths, "groups": groups, "image_map": image_map, "entry_weights": entry_weights, "exit_weights": exit_weights, "expand_weights": expand_weights, "contract_weights": contract_weights, "norm_gains": norm_gains, "entry_first": entry_first, "entry_second": entry_second, "exit_first": exit_first, "exit_second": exit_second, "expand_first": expand_first, "expand_second": expand_second, "contract_first": contract_first, "contract_second": contract_second, "gains_first": gains_first, "gains_second": gains_second}


group_scale = (1.0, 0.5, 2.0)
first_decay = 0.9
second_decay = 0.999
learn_rate = 0.5
weight_decay = 0.01
adam_eps = 1e-06
norm_eps = 1e-06
masked_score = -1e+30
highest = lax.Precision.HIGHEST

@jax.custom_vjp
def low(v):
    return lax.optimization_barrier(v.astype(jnp.bfloat16)).astype(jnp.float32)

@jax.custom_vjp
def low_back(v):
    return v

def low_keep(v):
    return (low(v), None)

def low_pass(kept, grad):
    return (grad,)

def back_keep(v):
    return (v, None)

def back_low(kept, grad):
    return (low(grad),)
low.defvjp(low_keep, low_pass)
low_back.defvjp(back_keep, back_low)

def token_layout(lengths, groups, image_map, tok_rows, img_count):
    text_count = lengths.shape[1]
    text_ends = jnp.cumsum(lengths, axis=1)
    position = jnp.arange(tok_rows, dtype=jnp.int32)
    segment = lax.optimization_barrier(jnp.sum((position[None, :, None] >= text_ends[:, None, :]).astype(jnp.int32), axis=2))
    chosen = (segment[:, :, None] == jnp.arange(text_count, dtype=jnp.int32)[None, None, :]).astype(jnp.int32)
    group_tok = lax.optimization_barrier(jnp.sum(chosen * groups[:, None, :], axis=2))
    image_tok = lax.optimization_barrier(jnp.sum(chosen * (image_map % img_count)[:, None, :], axis=2))
    scale_table = jnp.array(group_scale, dtype=jnp.float32)
    picked = (group_tok[:, :, None] == jnp.arange(3, dtype=jnp.int32)[None, None, :]).astype(jnp.float32)
    weight_tok = lax.optimization_barrier(jnp.sum(picked * scale_table, axis=2)) * (segment < text_count).astype(jnp.float32)
    return (segment, image_tok, weight_tok)

def rms_norm(values, gain):
    return values * lax.rsqrt(lax.optimization_barrier(jnp.mean(values * values, axis=-1, keepdims=True)) + norm_eps) * gain

def heads_attend(queries, key_rows, value_rows, allowed):
    score_scale = HEAD_DIM ** (-0.5)

    def one_head(parts):
        query_set, key_set, value_set = parts
        raw_scores = jnp.einsum('re,ke->rk', query_set, key_set, precision=highest)
        scores = jnp.where(allowed, low_back(raw_scores * score_scale), masked_score)
        probs = jax.nn.softmax(scores, axis=-1)
        return jnp.einsum('rk,ke->re', low(probs), value_set, precision=highest)
    result = lax.map(jax.checkpoint(one_head), (queries.transpose(1, 0, 2), key_rows.transpose(1, 0, 2), value_rows.transpose(1, 0, 2)))
    return result.transpose(1, 0, 2)

def self_stretch(parts):
    stacked, segment_row = parts
    position = jnp.arange(TOK_DEV, dtype=jnp.int32)
    allowed = (segment_row[:, None] == segment_row[None, :]) & (position[None, :] <= position[:, None])
    return heads_attend(stacked[:, 0], stacked[:, 1], stacked[:, 2], allowed)

def cross_stretch(parts):
    query_rows, pair_rows, image_rows = parts
    key_image = jnp.arange(IMG_DEV * PATCHES, dtype=jnp.int32) // PATCHES
    allowed = image_rows[:, None] == key_image[None, :]
    return heads_attend(query_rows, pair_rows[:, 0], pair_rows[:, 1], allowed)

def lamb_update(weight, grad, first, second, decay, axes):
    mean = first_decay * first + (1.0 - first_decay) * grad
    square = second_decay * second + (1.0 - second_decay) * grad * grad
    step = mean / (1.0 - first_decay ** STEPS_DONE) / (jnp.sqrt(square / (1.0 - second_decay ** STEPS_DONE)) + adam_eps) + decay * weight
    weight_norm = jnp.sqrt(lax.optimization_barrier(jnp.sum(weight * weight, axis=axes, keepdims=True)))
    step_norm = jnp.sqrt(lax.optimization_barrier(jnp.sum(step * step, axis=axes, keepdims=True)))
    fresh = weight - learn_rate * weight_norm / (step_norm + adam_eps) * step
    return (mean, square, fresh, weight_norm.reshape(-1), step_norm.reshape(-1))

def reference(tokens, memory, cotangent, lengths, groups, image_map, entry_weights, exit_weights, expand_weights, contract_weights, norm_gains, entry_first, entry_second, exit_first, exit_second, expand_first, expand_second, contract_first, contract_second, gains_first, gains_second):
    segment, image_tok, weight_tok = token_layout(lengths.reshape(N_DP, TEXT_DEV), groups.reshape(N_DP, TEXT_DEV), image_map.reshape(N_DP, TEXT_DEV), TOK_DEV, IMG_DEV)

    def forward(stream, memory_rows, entry_all, exit_all, expand_all, contract_all, gains_all):
        entry_low = low(entry_all)
        exit_low = low(exit_all)
        expand_low = low(expand_all)
        contract_low = low(contract_all)
        gains_low = low(gains_all)
        hidden_one = low(rms_norm(stream, gains_low[0]))
        projected = low_back(low(jnp.einsum('td,sdc->tsc', hidden_one, entry_low[0:3], precision=highest)))
        stacked = projected.reshape(N_DP, TOK_DEV, 3, HEADS, HEAD_DIM)
        self_out = lax.map(jax.checkpoint(self_stretch), (stacked, segment))
        self_flat = low_back(low(self_out.reshape(TOKENS, D)))
        stream_one = stream + low_back(jnp.dot(self_flat, exit_low[0], precision=highest))
        hidden_two = low(rms_norm(stream_one, gains_low[1]))
        cross_queries = low_back(low(jnp.dot(hidden_two, entry_low[3], precision=highest)))
        pairs = low_back(low(jnp.einsum('npd,sdc->npsc', memory_rows, entry_low[4:6], precision=highest)))
        pair_stretches = pairs.reshape(N_DP, IMG_DEV * PATCHES, 2, HEADS, HEAD_DIM)
        cross_out = lax.map(jax.checkpoint(cross_stretch), (cross_queries.reshape(N_DP, TOK_DEV, HEADS, HEAD_DIM), pair_stretches, image_tok))
        cross_flat = low_back(low(cross_out.reshape(TOKENS, D)))
        stream_two = stream_one + low_back(jnp.dot(cross_flat, exit_low[1], precision=highest))
        hidden_three = low(rms_norm(stream_two, gains_low[2]))
        gate_up = low_back(jnp.einsum('td,sdf->tsf', hidden_three, expand_low, precision=highest))
        activated = low(jax.nn.gelu(gate_up[:, 0], approximate=True) * gate_up[:, 1])
        return stream_two + low_back(jnp.dot(activated, contract_low, precision=highest))
    stream = tokens.astype(jnp.float32)
    memory_rows = memory.astype(jnp.float32)
    output, pullback = jax.vjp(forward, stream, memory_rows, entry_weights, exit_weights, expand_weights, contract_weights, norm_gains)
    weighted = cotangent.astype(jnp.float32) * weight_tok.reshape(TOKENS)[:, None]
    token_grads, memory_grads, entry_grads, exit_grads, expand_grads, contract_grads, gain_grads = pullback(weighted)
    entry_mean, entry_square, entry_new, entry_wn, entry_un = lamb_update(entry_weights, entry_grads, entry_first, entry_second, weight_decay, (1, 2))
    exit_mean, exit_square, exit_new, exit_wn, exit_un = lamb_update(exit_weights, exit_grads, exit_first, exit_second, weight_decay, (1, 2))
    expand_mean, expand_square, expand_new, expand_wn, expand_un = lamb_update(expand_weights, expand_grads, expand_first, expand_second, weight_decay, (1, 2))
    contract_mean, contract_square, contract_new, contract_wn, contract_un = lamb_update(contract_weights, contract_grads, contract_first, contract_second, weight_decay, (0, 1))
    gains_mean, gains_square, gains_new, gains_wn, gains_un = lamb_update(norm_gains, gain_grads, gains_first, gains_second, 0.0, (1,))
    trust_norms = jnp.stack([jnp.concatenate([entry_wn, exit_wn, expand_wn, contract_wn, gains_wn]), jnp.concatenate([entry_un, exit_un, expand_un, contract_un, gains_un])])
    return (output, token_grads, memory_grads, entry_grads, exit_grads, expand_grads, contract_grads, gain_grads, entry_mean, exit_mean, expand_mean, contract_mean, gains_mean, entry_square, exit_square, expand_square, contract_square, gains_square, entry_new, exit_new, expand_new, contract_new, gains_new, entry_new.astype(jnp.bfloat16), exit_new.astype(jnp.bfloat16), expand_new.astype(jnp.bfloat16), contract_new.astype(jnp.bfloat16), trust_norms)
```

```python
import jax
import jax.numpy as jnp
from jax import lax
from jax.experimental import pallas as pl
from jax.experimental.pallas import tpu as pltpu
from jax.sharding import PartitionSpec as P

HEAD_DIM = 64
IMG_DEV = 2
STEPS_DONE = 10


group_scale = (1.0, 0.5, 2.0)
first_decay = 0.9
second_decay = 0.999
learn_rate = 0.5
weight_decay = 0.01
adam_eps = 1e-06
norm_eps = 1e-06
masked_score = -1e30


def token_layout(lengths, groups, image_map, tok_rows, img_count):
    text_count = lengths.shape[1]
    text_ends = jnp.cumsum(lengths, axis=1)
    position = jnp.arange(tok_rows, dtype=jnp.int32)
    segment = jnp.sum((position[None, :, None] >= text_ends[:, None, :]).astype(jnp.int32), axis=2)
    chosen = (segment[:, :, None] == jnp.arange(text_count, dtype=jnp.int32)[None, None, :]).astype(
        jnp.int32
    )
    group_tok = jnp.sum(chosen * groups[:, None, :], axis=2)
    image_tok = jnp.sum(chosen * (image_map % img_count)[:, None, :], axis=2)
    scale_table = jnp.array(group_scale, dtype=jnp.float32)
    picked = (group_tok[:, :, None] == jnp.arange(3, dtype=jnp.int32)[None, None, :]).astype(
        jnp.float32
    )
    weight_tok = jnp.sum(picked * scale_table, axis=2) * (segment < text_count).astype(jnp.float32)
    return (segment, image_tok, weight_tok)


def rms_norm(values, gain):
    return values * lax.rsqrt(jnp.mean(values * values, axis=-1, keepdims=True) + norm_eps) * gain


def gated_hidden(gate, upward):
    return jax.nn.gelu(gate, approximate=True) * upward


BLOCK = 256
LANES = 128
LOG2E = 1.4426950408889634
NT = (((1,), (1,)), ((), ()))
TN = (((0,), (0,)), ((), ()))
VMEM_LIMIT = 50 * 1024 * 1024


def mm(a, b, dims=(((1,), (0,)), ((), ()))):
    return lax.dot_general(a, b, dims, preferred_element_type=jnp.float32)


def half_lanes(block, half):
    lane = lax.broadcasted_iota(jnp.int32, (1, LANES), 1)
    return jnp.where((lane // HEAD_DIM) == half, block, jnp.zeros_like(block))


def span_mask(start_ref, block, keys):
    low = block * BLOCK
    key_pos = lax.broadcasted_iota(jnp.int32, (keys, BLOCK), 0)
    query_pos = low + lax.broadcasted_iota(jnp.int32, (keys, BLOCK), 1)
    return (key_pos >= start_ref[0:1, low : low + BLOCK]) & (key_pos <= query_pos)


def self_forward_kernel(qkv_ref, start_ref, out_ref, sums_ref):
    rows = qkv_ref.shape[0]
    scale = HEAD_DIM ** (-0.5)
    sums_ref[...] = jnp.zeros_like(sums_ref)
    for pair in range(2):
        lanes = slice(LANES * pair, LANES * (pair + 1))
        for block in range(rows // BLOCK):
            own = slice(block * BLOCK, (block + 1) * BLOCK)
            keys = (block + 1) * BLOCK
            key_set = qkv_ref[0:keys, 256 + LANES * pair : 256 + LANES * (pair + 1)]
            value_set = qkv_ref[0:keys, 512 + LANES * pair : 512 + LANES * (pair + 1)]
            query_set = qkv_ref[own, lanes]
            allowed = span_mask(start_ref, block, keys)
            pieces = []
            for half in range(2 - pair):
                scores = mm(key_set, half_lanes(query_set, half), NT)
                scores = jnp.where(allowed, scores, masked_score)
                largest = jnp.max(scores, axis=0, keepdims=True)
                weights = jnp.exp2((scores - largest) * (scale * LOG2E))
                total = jnp.sum(weights, axis=0, keepdims=True)
                mixed = mm(value_set, weights.astype(jnp.bfloat16), TN) / total
                pieces.append(mixed[half * HEAD_DIM : (half + 1) * HEAD_DIM])
                row = 2 * pair + half
                sums_ref[row : row + 1, own] = largest * scale + jnp.log(total)
            if pair == 1:
                pieces.append(jnp.zeros_like(pieces[0]))
            out_ref[own, lanes] = jnp.concatenate(pieces, axis=0).T.astype(jnp.bfloat16)


def self_forward(qkv, starts):
    rows = qkv.shape[0]
    return pl.pallas_call(
        self_forward_kernel,
        out_shape=(
            jax.ShapeDtypeStruct((rows, 256), jnp.bfloat16),
            jax.ShapeDtypeStruct((8, rows), jnp.float32),
        ),
        compiler_params=pltpu.CompilerParams(vmem_limit_bytes=VMEM_LIMIT),
        cost_estimate=pl.CostEstimate(
            flops=3 * rows * rows * 256, bytes_accessed=rows * 2048, transcendentals=2 * rows * rows
        ),
        name="self_forward",
    )(qkv, starts)


def self_backward_kernel(
    qkv_ref, grad_ref, out_ref, sums_ref, start_ref, result_ref, key_acc, value_acc
):
    rows = qkv_ref.shape[0]
    scale = HEAD_DIM ** (-0.5)
    for pair in range(2):
        lanes = slice(LANES * pair, LANES * (pair + 1))
        key_lanes = slice(256 + LANES * pair, 256 + LANES * (pair + 1))
        value_lanes = slice(512 + LANES * pair, 512 + LANES * (pair + 1))
        for block in reversed(range(rows // BLOCK)):
            own = slice(block * BLOCK, (block + 1) * BLOCK)
            keys = (block + 1) * BLOCK
            key_set = qkv_ref[0:keys, key_lanes]
            value_set = qkv_ref[0:keys, value_lanes]
            query_set = qkv_ref[own, lanes]
            grad_set = grad_ref[own, lanes]
            allowed = span_mask(start_ref, block, keys)
            product = (
                grad_set.astype(jnp.float32) * out_ref[own, lanes].astype(jnp.float32)
            ).T
            pieces = []
            key_part = None
            for half in range(2 - pair):
                row = 2 * pair + half
                inner = jnp.sum(
                    product[half * HEAD_DIM : (half + 1) * HEAD_DIM], axis=0, keepdims=True
                )
                query_half = half_lanes(query_set, half)
                grad_half = half_lanes(grad_set, half)
                scores = mm(key_set, query_half, NT)
                probs = jnp.where(
                    allowed,
                    jnp.exp2(scores * (scale * LOG2E) - sums_ref[row : row + 1, own] * LOG2E),
                    0.0,
                )
                grad_probs = mm(value_set, grad_half, NT)
                grad_scores = (probs * (grad_probs - inner)).astype(jnp.bfloat16)
                value_new = mm(probs.astype(jnp.bfloat16), grad_half)
                key_new = mm(grad_scores, query_half)
                key_part = key_new if key_part is None else key_part + key_new
                value_part = value_new if half == 0 else value_part + value_new
                mixed = mm(key_set, grad_scores, TN) * scale
                pieces.append(mixed[half * HEAD_DIM : (half + 1) * HEAD_DIM])
            if pair == 1:
                pieces.append(jnp.zeros_like(pieces[0]))
            result_ref[own, lanes] = jnp.concatenate(pieces, axis=0).T.astype(jnp.bfloat16)
            if keys == rows:
                key_acc[...] = key_part
                value_acc[...] = value_part
            else:
                key_acc[0:keys, :] += key_part
                value_acc[0:keys, :] += value_part
        result_ref[:, key_lanes] = (key_acc[...] * scale).astype(jnp.bfloat16)
        result_ref[:, value_lanes] = value_acc[...].astype(jnp.bfloat16)


def self_backward(qkv, grad_out, out, sums, starts):
    rows = qkv.shape[0]
    return pl.pallas_call(
        self_backward_kernel,
        out_shape=jax.ShapeDtypeStruct((rows, 768), jnp.bfloat16),
        scratch_shapes=[
            pltpu.VMEM((rows, LANES), jnp.float32),
            pltpu.VMEM((rows, LANES), jnp.float32),
        ],
        compiler_params=pltpu.CompilerParams(vmem_limit_bytes=VMEM_LIMIT),
        cost_estimate=pl.CostEstimate(
            flops=3 * rows * rows * 640, bytes_accessed=rows * 5120, transcendentals=2 * rows * rows
        ),
        name="self_backward",
    )(qkv, grad_out, out, sums, starts)


def image_blocks(split, image, blocks):
    if image == 0:
        return 0, (split + BLOCK - 1) // BLOCK
    return split // BLOCK, blocks


def own_columns(split, image, low):
    column = low + lax.broadcasted_iota(jnp.int32, (1, BLOCK), 1)
    return column < split if image == 0 else column >= split


def own_rows(split, image, low):
    row = low + lax.broadcasted_iota(jnp.int32, (BLOCK, LANES), 0)
    return row < split if image == 0 else row >= split


def cross_forward_kernel(split_ref, query_ref, key_ref, value_ref, out_ref, sums_ref):
    rows = query_ref.shape[0]
    keys = key_ref.shape[0] // IMG_DEV
    scale = HEAD_DIM ** (-0.5)
    split = split_ref[0]
    for image in range(IMG_DEV):
        first, last = image_blocks(split, image, rows // BLOCK)

        def step(block, carry):
            low = pl.multiple_of(block * BLOCK, BLOCK)
            query_set = query_ref[pl.ds(low, BLOCK), :]
            key_set = key_ref[image * keys : (image + 1) * keys, :]
            value_set = value_ref[image * keys : (image + 1) * keys, :]
            kept = own_columns(split, image, low)
            pieces = []
            for half in range(2):
                scores = mm(key_set, half_lanes(query_set, half), NT)
                largest = jnp.max(scores, axis=0, keepdims=True)
                weights = jnp.exp2((scores - largest) * (scale * LOG2E))
                total = jnp.sum(weights, axis=0, keepdims=True)
                mixed = mm(value_set, weights.astype(jnp.bfloat16), TN) / total
                pieces.append(mixed[half * HEAD_DIM : (half + 1) * HEAD_DIM])
                held = sums_ref[0, half : half + 1, pl.ds(low, BLOCK)]
                sums_ref[0, half : half + 1, pl.ds(low, BLOCK)] = jnp.where(
                    kept, largest * scale + jnp.log(total), held
                )
            fresh = jnp.concatenate(pieces, axis=0).T
            held = out_ref[pl.ds(low, BLOCK), :].astype(jnp.float32)
            out_ref[pl.ds(low, BLOCK), :] = jnp.where(
                own_rows(split, image, low), fresh, held
            ).astype(jnp.bfloat16)
            return carry

        lax.fori_loop(first, last, step, 0)


def cross_forward(split, queries, pairs):
    rows, width = queries.shape
    keys = pairs.shape[0]
    groups = width // LANES
    return pl.pallas_call(
        cross_forward_kernel,
        grid=(groups,),
        in_specs=[
            pl.BlockSpec(memory_space=pltpu.SMEM),
            pl.BlockSpec((rows, LANES), lambda j: (0, j)),
            pl.BlockSpec((keys, LANES), lambda j: (0, j)),
            pl.BlockSpec((keys, LANES), lambda j: (0, groups + j)),
        ],
        out_specs=(
            pl.BlockSpec((rows, LANES), lambda j: (0, j)),
            pl.BlockSpec((1, 8, rows), lambda j: (j, 0, 0)),
        ),
        out_shape=(
            jax.ShapeDtypeStruct((rows, width), jnp.bfloat16),
            jax.ShapeDtypeStruct((groups, 8, rows), jnp.float32),
        ),
        compiler_params=pltpu.CompilerParams(vmem_limit_bytes=VMEM_LIMIT),
        cost_estimate=pl.CostEstimate(
            flops=groups * rows * keys * 512,
            bytes_accessed=keys * 1536,
            transcendentals=groups * rows * keys,
        ),
        name="cross_forward",
    )(split, queries, pairs, pairs)


def cross_backward_kernel(
    split_ref,
    query_ref,
    grad_ref,
    stats_ref,
    key_ref,
    value_ref,
    query_out,
    key_out,
    value_out,
    key_acc,
    value_acc,
):
    rows = query_ref.shape[0]
    keys = key_ref.shape[0] // IMG_DEV
    scale = HEAD_DIM ** (-0.5)
    split = split_ref[0]
    for image in range(IMG_DEV):
        first, last = image_blocks(split, image, rows // BLOCK)
        span = slice(image * keys, (image + 1) * keys)
        key_acc[...] = jnp.zeros_like(key_acc)
        value_acc[...] = jnp.zeros_like(value_acc)

        def step(block, carry):
            low = pl.multiple_of(block * BLOCK, BLOCK)
            query_set = query_ref[pl.ds(low, BLOCK), :]
            grad_set = grad_ref[pl.ds(low, BLOCK), :]
            key_set = key_ref[span, :]
            value_set = value_ref[span, :]
            kept = own_columns(split, image, low)
            pieces = []
            for half in range(2):
                sums = stats_ref[0, half : half + 1, pl.ds(low, BLOCK)]
                inner = stats_ref[0, 2 + half : 3 + half, pl.ds(low, BLOCK)]
                shift = jnp.where(kept, sums * LOG2E, -masked_score)
                query_half = half_lanes(query_set, half)
                grad_half = half_lanes(grad_set, half)
                scores = mm(key_set, query_half, NT)
                probs = jnp.exp2(scores * (scale * LOG2E) - shift)
                grad_probs = mm(value_set, grad_half, NT)
                grad_scores = (probs * (grad_probs - inner)).astype(jnp.bfloat16)
                value_new = mm(probs.astype(jnp.bfloat16), grad_half)
                key_new = mm(grad_scores, query_half)
                value_part = value_new if half == 0 else value_part + value_new
                key_part = key_new if half == 0 else key_part + key_new
                mixed = mm(key_set, grad_scores, TN) * scale
                pieces.append(mixed[half * HEAD_DIM : (half + 1) * HEAD_DIM])
            key_acc[...] += key_part
            value_acc[...] += value_part
            fresh = jnp.concatenate(pieces, axis=0).T
            held = query_out[pl.ds(low, BLOCK), :].astype(jnp.float32)
            query_out[pl.ds(low, BLOCK), :] = jnp.where(
                own_rows(split, image, low), fresh, held
            ).astype(jnp.bfloat16)
            return carry

        lax.fori_loop(first, last, step, 0)
        key_out[span, :] = (key_acc[...] * scale).astype(jnp.bfloat16)
        value_out[span, :] = value_acc[...].astype(jnp.bfloat16)


def cross_backward(split, queries, grads, stats, pairs):
    rows, width = queries.shape
    keys = pairs.shape[0]
    groups = width // LANES
    return pl.pallas_call(
        cross_backward_kernel,
        grid=(groups,),
        in_specs=[
            pl.BlockSpec(memory_space=pltpu.SMEM),
            pl.BlockSpec((rows, LANES), lambda j: (0, j)),
            pl.BlockSpec((rows, LANES), lambda j: (0, j)),
            pl.BlockSpec((1, 8, rows), lambda j: (j, 0, 0)),
            pl.BlockSpec((keys, LANES), lambda j: (0, j)),
            pl.BlockSpec((keys, LANES), lambda j: (0, groups + j)),
        ],
        out_specs=(
            pl.BlockSpec((rows, LANES), lambda j: (0, j)),
            pl.BlockSpec((keys, LANES), lambda j: (0, j)),
            pl.BlockSpec((keys, LANES), lambda j: (0, j)),
        ),
        out_shape=(
            jax.ShapeDtypeStruct((rows, width), jnp.bfloat16),
            jax.ShapeDtypeStruct((keys, width), jnp.bfloat16),
            jax.ShapeDtypeStruct((keys, width), jnp.bfloat16),
        ),
        scratch_shapes=[
            pltpu.VMEM((keys // IMG_DEV, LANES), jnp.float32),
            pltpu.VMEM((keys // IMG_DEV, LANES), jnp.float32),
        ],
        compiler_params=pltpu.CompilerParams(vmem_limit_bytes=VMEM_LIMIT),
        cost_estimate=pl.CostEstimate(
            flops=groups * rows * keys * 1280,
            bytes_accessed=keys * 3072,
            transcendentals=groups * rows * keys,
        ),
        name="cross_backward",
    )(split, queries, grads, stats, pairs, pairs)


def rms_pull(values, gain, grad):
    inverse = lax.rsqrt(jnp.mean(values * values, axis=-1, keepdims=True) + norm_eps)
    hat = values * inverse
    scaled = grad * gain
    inner = jnp.mean(scaled * hat, axis=-1, keepdims=True)
    return inverse * (scaled - hat * inner), jnp.sum(grad * hat, axis=0)


def head_swap(blocks):
    return lax.all_to_all(blocks, "head", split_axis=0, concat_axis=0, tiled=True)


def two_terms(values):
    high = lax.reduce_precision(values, exponent_bits=8, mantissa_bits=7)
    return high.astype(jnp.bfloat16), (values - high).astype(jnp.bfloat16)


def after(array, *earlier):
    return lax.optimization_barrier((array, *earlier))[0]


def head_spread(block):
    head_count = lax.axis_size("head")
    return head_swap(jnp.broadcast_to(block[None], (head_count, *block.shape)))


def lamb_step(weight, grad, first, second, decay):
    mean = first_decay * first + (1.0 - first_decay) * grad
    square = second_decay * second + (1.0 - second_decay) * grad * grad
    step = (
        mean
        / (1.0 - first_decay**STEPS_DONE)
        / (jnp.sqrt(square / (1.0 - second_decay**STEPS_DONE)) + adam_eps)
        + decay * weight
    )
    return (mean, square, step)


def per_device(
    tokens,
    memory,
    cotangent,
    lengths,
    groups,
    image_map,
    entry_weights,
    exit_weights,
    expand_weights,
    contract_weights,
    norm_gains,
    entry_first,
    entry_second,
    exit_first,
    exit_second,
    expand_first,
    expand_second,
    contract_first,
    contract_second,
    gains_first,
    gains_second,
):
    dp_count = lax.axis_size("dp")
    head_count = lax.axis_size("head")
    dp_index = lax.axis_index("dp")
    head_index = lax.axis_index("head")
    group = head_index % 2
    bf16 = jnp.bfloat16
    f32 = jnp.float32
    tok_rows, width = tokens.shape
    local = entry_weights.shape[2]
    hidden = expand_weights.shape[2]
    shard = width // dp_count
    row_count = tok_rows // head_count
    patch_local = memory.shape[1]
    patches = dp_count * patch_local
    heads = local // HEAD_DIM
    order = (0, 2, 1, 3)

    entry_low = entry_weights.astype(bf16).transpose(1, 0, 2)
    exit_low = exit_weights.astype(bf16).transpose(2, 0, 1)
    expand_low = expand_weights.astype(bf16).transpose(1, 0, 2)
    contract_low = contract_weights.astype(bf16).transpose(1, 0)[:, None]
    gains_low = jnp.pad(norm_gains.astype(bf16).transpose(1, 0), ((0, 0), (0, LANES - 3)))
    own_first = jnp.pad(entry_low[:, 0:3], ((0, 0), (0, 0), (0, 256 - local)))
    own_first = jnp.concatenate([own_first.reshape(shard, 768), gains_low], axis=1)
    first_set = jnp.concatenate([entry_low[:, 3:6], exit_low], axis=1)
    first_set = lax.all_gather(first_set, "head", axis=0)
    own_first = after(own_first, first_set)
    self_full = lax.all_gather(own_first, "dp", axis=0, tiled=True)
    self_weights = self_full[:, 0:768]
    gain_values = self_full[:, 768 : 768 + 3].astype(f32).transpose(1, 0)

    first_set = jnp.stack([first_set[h] for h in order], axis=2)
    natural = first_set[:, 3][:, (0, 2, 1, 3)]
    pair_set = first_set[:, 1:3].reshape(shard, 2, 2, 2 * local)
    pair_set = jnp.where(group == 0, pair_set[:, :, 0], pair_set[:, :, 1])
    first_set = jnp.concatenate(
        [
            natural.reshape(shard, width),
            first_set[:, 0].reshape(shard, width),
            pair_set.reshape(shard, width),
            first_set[:, 4].reshape(shard, width),
        ],
        axis=1,
    )
    first_full = lax.all_gather(first_set, "dp", axis=0, tiled=True)
    exit_self_t = first_full[:, 0:768]
    cross_query = first_full[:, 768:1536]
    cross_pair = first_full[:, 1536:2304]
    exit_cross_t = first_full[:, 2304:3072]

    images_here = memory.reshape(dp_count, IMG_DEV * patch_local, width)
    images_here = after(images_here, self_full)
    moved = lax.all_to_all(images_here, "dp", split_axis=0, concat_axis=0, tiled=True)
    moved = (
        moved.reshape(dp_count, IMG_DEV, patch_local, width)
        .transpose(1, 0, 2, 3)
        .reshape(IMG_DEV, patches, width)
    )
    near = [(s, s ^ 1) for s in range(head_count)]
    other = lax.ppermute(moved, "head", near)
    memory_pair = jnp.concatenate([moved, other], axis=1).reshape(2 * IMG_DEV * patches, width)

    second_set = jnp.concatenate([expand_low, contract_low], axis=1)
    second_set = head_spread(after(second_set, self_full))
    second_set = second_set.transpose(1, 2, 0, 3).reshape(shard, 3 * head_count * hidden)
    second_full = lax.all_gather(after(second_set, first_full), "dp", axis=0, tiled=True)
    inner_width = head_count * hidden
    gate_weights = second_full[:, 0:inner_width]
    up_weights = second_full[:, inner_width : 2 * inner_width]
    contract_t = second_full[:, 2 * inner_width :]

    segments, images, weights = token_layout(
        lengths.reshape(1, -1), groups.reshape(1, -1), image_map.reshape(1, -1), tok_rows, IMG_DEV
    )
    image_tok = images[0]
    weight_tok = weights[0]
    text_ends = jnp.cumsum(lengths)
    position = jnp.arange(tok_rows, dtype=jnp.int32)
    starts = jnp.max(
        jnp.where(position[None, :] >= text_ends[:, None], text_ends[:, None], 0), axis=0
    ).reshape(1, tok_rows)
    of_zero = (image_tok == 0).astype(jnp.int32)
    before = jnp.cumsum(of_zero)
    split = before[-1]
    place = jnp.where(image_tok == 0, before - 1, split + position - before)
    sorter = (place[None, :] == position[:, None]).astype(bf16)
    unsorter = (place[:, None] == position[None, :]).astype(bf16)
    split = split.reshape(1)

    def own(array):
        return lax.dynamic_slice_in_dim(array, head_index * row_count, row_count)

    stream = tokens.astype(f32)
    hidden_one = rms_norm(stream, gain_values[0]).astype(bf16)
    qkv = mm(hidden_one, self_weights).astype(bf16)
    self_out, self_sums = self_forward(qkv, starts)
    self_rows = head_swap(self_out[:, 0:local].reshape(head_count, row_count, local))
    self_rows = self_rows.transpose(1, 0, 2).reshape(row_count, width)
    stream_rows = own(stream)
    stream_one = stream_rows + mm(self_rows, exit_self_t, NT)
    hidden_two = rms_norm(stream_one, gain_values[1]).astype(bf16)

    def to_groups(rows):
        pieces = [rows[:, 0 : width // 2], rows[:, width // 2 :]]
        return jnp.stack(pieces + pieces)

    query_rows = mm(hidden_two, cross_query).astype(bf16)
    queries = head_swap(to_groups(query_rows)).reshape(tok_rows, width // 2)
    queries = mm(sorter, queries).astype(bf16)
    pairs = mm(memory_pair, cross_pair).astype(bf16)
    cross_out, cross_sums = cross_forward(split, queries, pairs)
    cross_out = mm(unsorter, cross_out).astype(bf16)
    high, low = two_terms(cross_sums[:, 0:2].reshape(2 * heads, tok_rows))
    tail = jnp.concatenate([high, low, jnp.zeros((4, tok_rows), bf16)], axis=0)
    tail = mm(tail, sorter).astype(bf16)
    tail = tail.reshape(16, head_count, row_count).transpose(1, 0, 2)
    tail = jnp.pad(tail, ((0, 0), (0, 0), (0, width // 2 - row_count)))
    sending = jnp.concatenate(
        [cross_out.reshape(head_count, row_count, width // 2), tail], axis=1
    )
    got = head_swap(sending)
    spread = (
        jnp.arange(2 * heads)[:, None] == (jnp.arange(width // 2) // HEAD_DIM)[None, :]
    ).astype(f32)

    def lanes_of(per_head):
        return lax.dot_general(
            per_head, spread, TN, precision=lax.Precision.HIGHEST, preferred_element_type=f32
        )

    merged = []
    merged_sums = []
    for g in range(2):
        part = [got[g], got[g + 2]]
        sums = [
            p[row_count : row_count + 2 * heads, 0:row_count].astype(f32)
            + p[row_count + 2 * heads : row_count + 4 * heads, 0:row_count].astype(f32)
            for p in part
        ]
        largest = jnp.maximum(sums[0], sums[1])
        both = [jnp.exp(s - largest) for s in sums]
        total = both[0] + both[1]
        merged.append(
            lanes_of(both[0] / total) * part[0][0:row_count].astype(f32)
            + lanes_of(both[1] / total) * part[1][0:row_count].astype(f32)
        )
        merged_sums.append(largest + jnp.log(total))
    cross_rows = jnp.concatenate(merged, axis=1).astype(bf16)
    stream_two = stream_one + mm(cross_rows, exit_cross_t, NT)
    hidden_three = rms_norm(stream_two, gain_values[2]).astype(bf16)

    gate = mm(hidden_three, gate_weights)
    upward = mm(hidden_three, up_weights)
    activated, pull_gate = jax.vjp(gated_hidden, gate, upward)
    activated_low = activated.astype(bf16)
    output_rows = stream_two + mm(activated_low, contract_t, NT)
    grad_rows = own(cotangent).astype(f32) * own(weight_tok)[:, None]
    grad_low = grad_rows.astype(bf16)
    grad_gate, grad_up = pull_gate(mm(grad_low, contract_t))
    grad_gate = grad_gate.astype(bf16)
    grad_up = grad_up.astype(bf16)
    grad_normed = mm(grad_gate, gate_weights, NT) + mm(grad_up, up_weights, NT)
    second_part = jnp.concatenate(
        [
            mm(hidden_three, grad_gate, TN).astype(bf16),
            mm(hidden_three, grad_up, TN).astype(bf16),
            mm(grad_low, activated_low, TN).astype(bf16),
        ],
        axis=1,
    )
    grad_input, gain_three = rms_pull(stream_two, gain_values[2], grad_normed)
    grad_rows = grad_rows + grad_input

    second_grads = lax.psum_scatter(second_part, "dp", scatter_dimension=0, tiled=True)

    grad_low = grad_rows.astype(bf16)
    exit_cross_part = mm(grad_low, cross_rows, TN).astype(bf16)
    grad_cross = mm(grad_low, exit_cross_t).astype(bf16)
    product = grad_cross.astype(f32) * cross_rows.astype(f32)
    tails = []
    for g in range(2):
        inner = lax.dot_general(
            spread,
            product[:, g * (width // 2) : (g + 1) * (width // 2)],
            NT,
            precision=lax.Precision.HIGHEST,
            preferred_element_type=f32,
        )
        tails.append(jnp.concatenate([*two_terms(merged_sums[g]), *two_terms(inner)], axis=0))
    tail = jnp.stack(tails + tails)
    tail = jnp.pad(tail, ((0, 0), (0, 32 - 8 * heads), (0, width // 2 - row_count)))
    got = head_swap(jnp.concatenate([to_groups(grad_cross), tail], axis=1))
    grads = mm(sorter, got[:, 0:row_count].reshape(tok_rows, width // 2)).astype(bf16)
    stats = (
        got[:, row_count : row_count + 8 * heads, 0:row_count]
        .transpose(1, 0, 2)
        .reshape(8 * heads, tok_rows)
    )
    stats = mm(stats, unsorter)
    sums = (stats[0 : 2 * heads] + stats[2 * heads : 4 * heads]).reshape(heads, 2, tok_rows)
    inner = (stats[4 * heads : 6 * heads] + stats[6 * heads :]).reshape(heads, 2, tok_rows)
    stats = jnp.concatenate([sums, inner, jnp.zeros((heads, 4, tok_rows), f32)], axis=1)
    grad_query, grad_key, grad_value = cross_backward(split, queries, grads, stats, pairs)
    grad_query = mm(unsorter, grad_query).astype(bf16)
    got = head_swap(grad_query.reshape(head_count, row_count, width // 2)).astype(f32)
    grad_query = jnp.concatenate([got[0] + got[2], got[1] + got[3]], axis=1).astype(bf16)
    query_part = mm(hidden_two, grad_query, TN).astype(bf16)
    grad_input, gain_two = rms_pull(
        stream_one, gain_values[1], mm(grad_query, cross_query, NT)
    )
    grad_rows = grad_rows + grad_input

    grad_pair = jnp.concatenate([grad_key, grad_value], axis=1)
    pair_part = mm(memory_pair, grad_pair, TN).astype(bf16)
    memory_part = mm(grad_pair, cross_pair, NT).reshape(IMG_DEV, 2, patches, width)
    returned = lax.ppermute(memory_part[:, 1].astype(bf16), "head", near)
    memory_sum = (memory_part[:, 0] + returned.astype(f32)).astype(bf16)
    memory_sum = (
        memory_sum.reshape(IMG_DEV, dp_count, patch_local, width)
        .transpose(1, 0, 2, 3)
        .reshape(dp_count, IMG_DEV * patch_local, width)
    )
    memory_grads = lax.all_to_all(memory_sum, "dp", split_axis=0, concat_axis=0, tiled=True)
    memory_grads = memory_grads.reshape(memory.shape).astype(f32)

    grad_low = grad_rows.astype(bf16)
    exit_self_part = mm(grad_low, self_rows, TN).astype(bf16)
    grad_self = mm(grad_low, exit_self_t).astype(bf16)
    grad_self = after(grad_self, second_grads)
    grad_self = head_swap(grad_self.reshape(row_count, head_count, local).transpose(1, 0, 2))
    grad_self = jnp.pad(grad_self.reshape(tok_rows, local), ((0, 0), (0, 256 - local)))
    grad_qkv = self_backward(qkv, grad_self, self_out, self_sums, starts)
    self_part = mm(hidden_one, grad_qkv, TN)
    grad_normed = mm(grad_qkv, self_weights, NT)
    inverse = lax.rsqrt(jnp.mean(stream * stream, axis=-1, keepdims=True) + norm_eps)
    gain_one = jnp.sum(grad_normed * stream * inverse, axis=0)
    grad_normed = head_swap(
        grad_normed.astype(bf16).reshape(head_count, row_count, width)
    ).astype(f32)
    grad_normed = jnp.sum(grad_normed, axis=0)
    grad_input, _ = rms_pull(stream_rows, gain_values[0], grad_normed)
    grad_rows = grad_rows + grad_input
    token_grads = head_spread(grad_rows.astype(bf16)).reshape(tok_rows, width).astype(f32)
    output = head_spread(output_rows.astype(bf16)).reshape(tok_rows, width).astype(f32)

    second_grads = second_grads.reshape(shard, 3, head_count, hidden).transpose(2, 0, 1, 3)
    second_grads = jnp.sum(head_swap(second_grads).astype(f32), axis=0)
    expand_grads = second_grads[:, 0:2].transpose(1, 0, 2)
    contract_grads = second_grads[:, 2].transpose(1, 0)

    first_part = jnp.concatenate([exit_self_part, query_part, pair_part, exit_cross_part], axis=1)
    first_grads = lax.psum_scatter(first_part, "dp", scatter_dimension=0, tiled=True)
    sets = first_grads.reshape(shard, 4, head_count, local)
    blocks = []
    for h in range(head_count):
        slot = order.index(h)
        mine = sets[:, 2].reshape(shard, 2, 2, local)[:, :, slot % 2]
        mine = jnp.where(group == h % 2, mine, jnp.zeros_like(mine))
        blocks.append(
            jnp.concatenate(
                [sets[:, 1, slot][:, None], mine, sets[:, 0, h][:, None], sets[:, 3, slot][:, None]],
                axis=1,
            )
        )
    first_grads = jnp.sum(head_swap(jnp.stack(blocks)).astype(f32), axis=0)
    exit_grads = first_grads[:, 3:5].transpose(1, 2, 0)

    gain_part = jnp.stack([gain_one, gain_two, gain_three])
    self_part = self_part.reshape(width, 3, 256)[:, :, 0:local].reshape(width, 3 * local)
    high, low = two_terms(gain_part.transpose(1, 0))
    self_part = jnp.concatenate([self_part.astype(bf16), high, low], axis=1)
    self_part = jnp.pad(self_part, ((0, 0), (0, 58)))
    self_grads = lax.all_to_all(
        self_part.reshape(dp_count, shard, -1), "dp", split_axis=0, concat_axis=0, tiled=True
    )
    self_grads = jnp.sum(self_grads.astype(f32), axis=0)
    gain_grads = self_grads[:, 3 * local : 3 * local + 3] + self_grads[:, 3 * local + 3 : 3 * local + 6]
    gain_grads = lax.psum(gain_grads, "head").transpose(1, 0)
    entry_grads = jnp.concatenate(
        [self_grads[:, 0 : 3 * local].reshape(shard, 3, local), first_grads[:, 0:3]], axis=1
    ).transpose(1, 0, 2)

    entry_mean, entry_square, entry_step = lamb_step(
        entry_weights, entry_grads, entry_first, entry_second, weight_decay
    )
    exit_mean, exit_square, exit_step = lamb_step(
        exit_weights, exit_grads, exit_first, exit_second, weight_decay
    )
    expand_mean, expand_square, expand_step = lamb_step(
        expand_weights, expand_grads, expand_first, expand_second, weight_decay
    )
    contract_mean, contract_square, contract_step = lamb_step(
        contract_weights, contract_grads, contract_first, contract_second, weight_decay
    )
    gains_mean, gains_square, gains_step = lamb_step(
        norm_gains, gain_grads, gains_first, gains_second, 0.0
    )
    weight_local = jnp.concatenate(
        [
            jnp.sum(entry_weights * entry_weights, axis=(1, 2)),
            jnp.sum(exit_weights * exit_weights, axis=(1, 2)),
            jnp.sum(expand_weights * expand_weights, axis=(1, 2)),
            jnp.sum(contract_weights * contract_weights).reshape(1),
            jnp.sum(norm_gains * norm_gains, axis=1) / head_count,
        ]
    )
    step_local = jnp.concatenate(
        [
            jnp.sum(entry_step * entry_step, axis=(1, 2)),
            jnp.sum(exit_step * exit_step, axis=(1, 2)),
            jnp.sum(expand_step * expand_step, axis=(1, 2)),
            jnp.sum(contract_step * contract_step).reshape(1),
            jnp.sum(gains_step * gains_step, axis=1) / head_count,
        ]
    )
    weight_squares, step_squares = lax.psum(lax.psum(jnp.stack([weight_local, step_local]), "dp"), "head")
    weight_norm = jnp.sqrt(weight_squares)
    step_norm = jnp.sqrt(step_squares)
    ratio = learn_rate * weight_norm / (step_norm + adam_eps)
    entry_new = entry_weights - ratio[0:6][:, None, None] * entry_step
    exit_new = exit_weights - ratio[6:8][:, None, None] * exit_step
    expand_new = expand_weights - ratio[8:10][:, None, None] * expand_step
    contract_new = contract_weights - ratio[10] * contract_step
    gains_new = norm_gains - ratio[11:14][:, None] * gains_step
    trust_norms = jnp.stack([weight_norm, step_norm])
    return (
        output,
        token_grads,
        memory_grads,
        entry_grads,
        exit_grads,
        expand_grads,
        contract_grads,
        gain_grads,
        entry_mean,
        exit_mean,
        expand_mean,
        contract_mean,
        gains_mean,
        entry_square,
        exit_square,
        expand_square,
        contract_square,
        gains_square,
        entry_new,
        exit_new,
        expand_new,
        contract_new,
        gains_new,
        entry_new.astype(jnp.bfloat16),
        exit_new.astype(jnp.bfloat16),
        expand_new.astype(jnp.bfloat16),
        contract_new.astype(jnp.bfloat16),
        trust_norms,
    )


def solution(mesh):
    in_specs = (
        P("dp", None),
        P(None, ("dp", "head"), None),
        P("dp", None),
        P("dp"),
        P("dp"),
        P("dp"),
        P(None, "dp", "head"),
        P(None, "head", "dp"),
        P(None, "dp", "head"),
        P("head", "dp"),
        P(None, "dp"),
        P(None, "dp", "head"),
        P(None, "dp", "head"),
        P(None, "head", "dp"),
        P(None, "head", "dp"),
        P(None, "dp", "head"),
        P(None, "dp", "head"),
        P("head", "dp"),
        P("head", "dp"),
        P(None, "dp"),
        P(None, "dp"),
    )
    out_specs = (
        P("dp", None),
        P("dp", None),
        P(None, ("dp", "head"), None),
        P(None, "dp", "head"),
        P(None, "head", "dp"),
        P(None, "dp", "head"),
        P("head", "dp"),
        P(None, "dp"),
        P(None, "dp", "head"),
        P(None, "head", "dp"),
        P(None, "dp", "head"),
        P("head", "dp"),
        P(None, "dp"),
        P(None, "dp", "head"),
        P(None, "head", "dp"),
        P(None, "dp", "head"),
        P("head", "dp"),
        P(None, "dp"),
        P(None, "dp", "head"),
        P(None, "head", "dp"),
        P(None, "dp", "head"),
        P("head", "dp"),
        P(None, "dp"),
        P(None, "dp", "head"),
        P(None, "head", "dp"),
        P(None, "dp", "head"),
        P("head", "dp"),
        P(),
    )
    return jax.shard_map(
        per_device, mesh=mesh, in_specs=in_specs, out_specs=out_specs, check_vma=False
    )
```

```python
import jax
import jax.numpy as jnp
from jax import lax
from jax.experimental import pallas as pl
from jax.experimental.pallas import tpu as pltpu
from jax.sharding import PartitionSpec as P

HEAD_DIM = 64
IMG_DEV = 2
STEPS_DONE = 10


group_scale = (1.0, 0.5, 2.0)
first_decay = 0.9
second_decay = 0.999
learn_rate = 0.5
weight_decay = 0.01
adam_eps = 1e-06
norm_eps = 1e-06
masked_score = -1e30


def token_layout(lengths, groups, image_map, tok_rows, img_count):
    text_count = lengths.shape[1]
    text_ends = jnp.cumsum(lengths, axis=1)
    position = jnp.arange(tok_rows, dtype=jnp.int32)
    segment = jnp.sum((position[None, :, None] >= text_ends[:, None, :]).astype(jnp.int32), axis=2)
    chosen = (segment[:, :, None] == jnp.arange(text_count, dtype=jnp.int32)[None, None, :]).astype(
        jnp.int32
    )
    group_tok = jnp.sum(chosen * groups[:, None, :], axis=2)
    image_tok = jnp.sum(chosen * (image_map % img_count)[:, None, :], axis=2)
    scale_table = jnp.array(group_scale, dtype=jnp.float32)
    picked = (group_tok[:, :, None] == jnp.arange(3, dtype=jnp.int32)[None, None, :]).astype(
        jnp.float32
    )
    weight_tok = jnp.sum(picked * scale_table, axis=2) * (segment < text_count).astype(jnp.float32)
    return (segment, image_tok, weight_tok)


def rms_norm(values, gain):
    return values * lax.rsqrt(jnp.mean(values * values, axis=-1, keepdims=True) + norm_eps) * gain


def gated_hidden(gate, upward):
    return jax.nn.gelu(gate, approximate=True) * upward


BLOCK = 256
LANES = 128
LOG2E = 1.4426950408889634
NT = (((1,), (1,)), ((), ()))
TN = (((0,), (0,)), ((), ()))
VMEM_LIMIT = 50 * 1024 * 1024


def mm(a, b, dims=(((1,), (0,)), ((), ()))):
    return lax.dot_general(a, b, dims, preferred_element_type=jnp.float32)


def half_lanes(block, half):
    lane = lax.broadcasted_iota(jnp.int32, (1, LANES), 1)
    return jnp.where((lane // HEAD_DIM) == half, block, jnp.zeros_like(block))


def span_mask(start_ref, block, keys):
    low = block * BLOCK
    key_pos = lax.broadcasted_iota(jnp.int32, (keys, BLOCK), 0)
    query_pos = low + lax.broadcasted_iota(jnp.int32, (keys, BLOCK), 1)
    return (key_pos >= start_ref[0:1, low : low + BLOCK]) & (key_pos <= query_pos)


def self_forward_kernel(qkv_ref, start_ref, out_ref, sums_ref):
    rows = qkv_ref.shape[0]
    scale = HEAD_DIM ** (-0.5)
    sums_ref[...] = jnp.zeros_like(sums_ref)
    for pair in range(2):
        lanes = slice(LANES * pair, LANES * (pair + 1))
        for block in range(rows // BLOCK):
            own = slice(block * BLOCK, (block + 1) * BLOCK)
            keys = (block + 1) * BLOCK
            key_set = qkv_ref[0:keys, 256 + LANES * pair : 256 + LANES * (pair + 1)]
            value_set = qkv_ref[0:keys, 512 + LANES * pair : 512 + LANES * (pair + 1)]
            query_set = qkv_ref[own, lanes]
            allowed = span_mask(start_ref, block, keys)
            pieces = []
            for half in range(2 - pair):
                scores = mm(key_set, half_lanes(query_set, half), NT)
                scores = jnp.where(allowed, scores, masked_score)
                largest = jnp.max(scores, axis=0, keepdims=True)
                weights = jnp.exp2((scores - largest) * (scale * LOG2E))
                total = jnp.sum(weights, axis=0, keepdims=True)
                mixed = mm(value_set, weights.astype(jnp.bfloat16), TN) / total
                pieces.append(mixed[half * HEAD_DIM : (half + 1) * HEAD_DIM])
                row = 2 * pair + half
                sums_ref[row : row + 1, own] = largest * scale + jnp.log(total)
            if pair == 1:
                pieces.append(jnp.zeros_like(pieces[0]))
            out_ref[own, lanes] = jnp.concatenate(pieces, axis=0).T.astype(jnp.bfloat16)


def self_forward(qkv, starts):
    rows = qkv.shape[0]
    return pl.pallas_call(
        self_forward_kernel,
        out_shape=(
            jax.ShapeDtypeStruct((rows, 256), jnp.bfloat16),
            jax.ShapeDtypeStruct((8, rows), jnp.float32),
        ),
        compiler_params=pltpu.CompilerParams(vmem_limit_bytes=VMEM_LIMIT),
        cost_estimate=pl.CostEstimate(
            flops=6 * 10**9, bytes_accessed=rows * 2048, transcendentals=2 * rows * rows
        ),
        name="self_forward",
    )(qkv, starts)


def self_backward_kernel(
    qkv_ref, grad_ref, out_ref, sums_ref, start_ref, result_ref, key_acc, value_acc
):
    rows = qkv_ref.shape[0]
    scale = HEAD_DIM ** (-0.5)
    for pair in range(2):
        lanes = slice(LANES * pair, LANES * (pair + 1))
        key_lanes = slice(256 + LANES * pair, 256 + LANES * (pair + 1))
        value_lanes = slice(512 + LANES * pair, 512 + LANES * (pair + 1))
        for block in reversed(range(rows // BLOCK)):
            own = slice(block * BLOCK, (block + 1) * BLOCK)
            keys = (block + 1) * BLOCK
            key_set = qkv_ref[0:keys, key_lanes]
            value_set = qkv_ref[0:keys, value_lanes]
            query_set = qkv_ref[own, lanes]
            grad_set = grad_ref[own, lanes]
            allowed = span_mask(start_ref, block, keys)
            product = (
                grad_set.astype(jnp.float32) * out_ref[own, lanes].astype(jnp.float32)
            ).T
            pieces = []
            key_part = None
            for half in range(2 - pair):
                row = 2 * pair + half
                inner = jnp.sum(
                    product[half * HEAD_DIM : (half + 1) * HEAD_DIM], axis=0, keepdims=True
                )
                query_half = half_lanes(query_set, half)
                grad_half = half_lanes(grad_set, half)
                scores = mm(key_set, query_half, NT)
                probs = jnp.where(
                    allowed,
                    jnp.exp2(scores * (scale * LOG2E) - sums_ref[row : row + 1, own] * LOG2E),
                    0.0,
                )
                grad_probs = mm(value_set, grad_half, NT)
                grad_scores = (probs * (grad_probs - inner)).astype(jnp.bfloat16)
                value_new = mm(probs.astype(jnp.bfloat16), grad_half)
                key_new = mm(grad_scores, query_half)
                key_part = key_new if key_part is None else key_part + key_new
                value_part = value_new if half == 0 else value_part + value_new
                mixed = mm(key_set, grad_scores, TN) * scale
                pieces.append(mixed[half * HEAD_DIM : (half + 1) * HEAD_DIM])
            if pair == 1:
                pieces.append(jnp.zeros_like(pieces[0]))
            result_ref[own, lanes] = jnp.concatenate(pieces, axis=0).T.astype(jnp.bfloat16)
            if keys == rows:
                key_acc[...] = key_part
                value_acc[...] = value_part
            else:
                key_acc[0:keys, :] += key_part
                value_acc[0:keys, :] += value_part
        result_ref[:, key_lanes] = (key_acc[...] * scale).astype(jnp.bfloat16)
        result_ref[:, value_lanes] = value_acc[...].astype(jnp.bfloat16)


def self_backward(qkv, grad_out, out, sums, starts):
    rows = qkv.shape[0]
    return pl.pallas_call(
        self_backward_kernel,
        out_shape=jax.ShapeDtypeStruct((rows, 768), jnp.bfloat16),
        scratch_shapes=[
            pltpu.VMEM((rows, LANES), jnp.float32),
            pltpu.VMEM((rows, LANES), jnp.float32),
        ],
        compiler_params=pltpu.CompilerParams(vmem_limit_bytes=VMEM_LIMIT),
        cost_estimate=pl.CostEstimate(
            flops=8 * 10**9, bytes_accessed=rows * 5120, transcendentals=2 * rows * rows
        ),
        name="self_backward",
    )(qkv, grad_out, out, sums, starts)


def image_blocks(split, image, blocks):
    if image == 0:
        return 0, (split + BLOCK - 1) // BLOCK
    return split // BLOCK, blocks


def own_columns(split, image, low):
    column = low + lax.broadcasted_iota(jnp.int32, (1, BLOCK), 1)
    return column < split if image == 0 else column >= split


def own_rows(split, image, low):
    row = low + lax.broadcasted_iota(jnp.int32, (BLOCK, LANES), 0)
    return row < split if image == 0 else row >= split


def cross_forward_kernel(split_ref, query_ref, key_ref, value_ref, out_ref, sums_ref):
    rows = query_ref.shape[0]
    keys = key_ref.shape[0] // IMG_DEV
    scale = HEAD_DIM ** (-0.5)
    split = split_ref[0]
    for image in range(IMG_DEV):
        first, last = image_blocks(split, image, rows // BLOCK)

        def step(block, carry):
            low = pl.multiple_of(block * BLOCK, BLOCK)
            query_set = query_ref[pl.ds(low, BLOCK), :]
            key_set = key_ref[image * keys : (image + 1) * keys, :]
            value_set = value_ref[image * keys : (image + 1) * keys, :]
            kept = own_columns(split, image, low)
            pieces = []
            for half in range(2):
                scores = mm(key_set, half_lanes(query_set, half), NT)
                largest = jnp.max(scores, axis=0, keepdims=True)
                weights = jnp.exp2((scores - largest) * (scale * LOG2E))
                total = jnp.sum(weights, axis=0, keepdims=True)
                mixed = mm(value_set, weights.astype(jnp.bfloat16), TN) / total
                pieces.append(mixed[half * HEAD_DIM : (half + 1) * HEAD_DIM])
                held = sums_ref[0, half : half + 1, pl.ds(low, BLOCK)]
                sums_ref[0, half : half + 1, pl.ds(low, BLOCK)] = jnp.where(
                    kept, largest * scale + jnp.log(total), held
                )
            fresh = jnp.concatenate(pieces, axis=0).T
            held = out_ref[pl.ds(low, BLOCK), :].astype(jnp.float32)
            out_ref[pl.ds(low, BLOCK), :] = jnp.where(
                own_rows(split, image, low), fresh, held
            ).astype(jnp.bfloat16)
            return carry

        lax.fori_loop(first, last, step, 0)


def cross_forward(split, queries, pairs):
    rows, width = queries.shape
    keys = pairs.shape[0]
    groups = width // LANES
    return pl.pallas_call(
        cross_forward_kernel,
        grid=(groups,),
        in_specs=[
            pl.BlockSpec(memory_space=pltpu.SMEM),
            pl.BlockSpec((rows, LANES), lambda j: (0, j)),
            pl.BlockSpec((keys, LANES), lambda j: (0, j)),
            pl.BlockSpec((keys, LANES), lambda j: (0, groups + j)),
        ],
        out_specs=(
            pl.BlockSpec((rows, LANES), lambda j: (0, j)),
            pl.BlockSpec((1, 8, rows), lambda j: (j, 0, 0)),
        ),
        out_shape=(
            jax.ShapeDtypeStruct((rows, width), jnp.bfloat16),
            jax.ShapeDtypeStruct((groups, 8, rows), jnp.float32),
        ),
        compiler_params=pltpu.CompilerParams(vmem_limit_bytes=VMEM_LIMIT),
        cost_estimate=pl.CostEstimate(
            flops=28 * 10**9,
            bytes_accessed=keys * 1536,
            transcendentals=groups * rows * keys,
        ),
        name="cross_forward",
    )(split, queries, pairs, pairs)


def cross_backward_kernel(
    split_ref,
    query_ref,
    grad_ref,
    stats_ref,
    key_ref,
    value_ref,
    query_out,
    key_out,
    value_out,
    key_acc,
    value_acc,
):
    rows = query_ref.shape[0]
    keys = key_ref.shape[0] // IMG_DEV
    scale = HEAD_DIM ** (-0.5)
    split = split_ref[0]
    for image in range(IMG_DEV):
        first, last = image_blocks(split, image, rows // BLOCK)
        span = slice(image * keys, (image + 1) * keys)
        key_acc[...] = jnp.zeros_like(key_acc)
        value_acc[...] = jnp.zeros_like(value_acc)

        def step(block, carry):
            low = pl.multiple_of(block * BLOCK, BLOCK)
            query_set = query_ref[pl.ds(low, BLOCK), :]
            grad_set = grad_ref[pl.ds(low, BLOCK), :]
            key_set = key_ref[span, :]
            value_set = value_ref[span, :]
            kept = own_columns(split, image, low)
            pieces = []
            for half in range(2):
                sums = stats_ref[0, half : half + 1, pl.ds(low, BLOCK)]
                inner = stats_ref[0, 2 + half : 3 + half, pl.ds(low, BLOCK)]
                shift = jnp.where(kept, sums * LOG2E, -masked_score)
                query_half = half_lanes(query_set, half)
                grad_half = half_lanes(grad_set, half)
                scores = mm(key_set, query_half, NT)
                probs = jnp.exp2(scores * (scale * LOG2E) - shift)
                grad_probs = mm(value_set, grad_half, NT)
                grad_scores = (probs * (grad_probs - inner)).astype(jnp.bfloat16)
                value_new = mm(probs.astype(jnp.bfloat16), grad_half)
                key_new = mm(grad_scores, query_half)
                value_part = value_new if half == 0 else value_part + value_new
                key_part = key_new if half == 0 else key_part + key_new
                mixed = mm(key_set, grad_scores, TN) * scale
                pieces.append(mixed[half * HEAD_DIM : (half + 1) * HEAD_DIM])
            key_acc[...] += key_part
            value_acc[...] += value_part
            fresh = jnp.concatenate(pieces, axis=0).T
            held = query_out[pl.ds(low, BLOCK), :].astype(jnp.float32)
            query_out[pl.ds(low, BLOCK), :] = jnp.where(
                own_rows(split, image, low), fresh, held
            ).astype(jnp.bfloat16)
            return carry

        lax.fori_loop(first, last, step, 0)
        key_out[span, :] = (key_acc[...] * scale).astype(jnp.bfloat16)
        value_out[span, :] = value_acc[...].astype(jnp.bfloat16)


def cross_backward(split, queries, grads, stats, pairs):
    rows, width = queries.shape
    keys = pairs.shape[0]
    groups = width // LANES
    return pl.pallas_call(
        cross_backward_kernel,
        grid=(groups,),
        in_specs=[
            pl.BlockSpec(memory_space=pltpu.SMEM),
            pl.BlockSpec((rows, LANES), lambda j: (0, j)),
            pl.BlockSpec((rows, LANES), lambda j: (0, j)),
            pl.BlockSpec((1, 8, rows), lambda j: (j, 0, 0)),
            pl.BlockSpec((keys, LANES), lambda j: (0, j)),
            pl.BlockSpec((keys, LANES), lambda j: (0, groups + j)),
        ],
        out_specs=(
            pl.BlockSpec((rows, LANES), lambda j: (0, j)),
            pl.BlockSpec((keys, LANES), lambda j: (0, j)),
            pl.BlockSpec((keys, LANES), lambda j: (0, j)),
        ),
        out_shape=(
            jax.ShapeDtypeStruct((rows, width), jnp.bfloat16),
            jax.ShapeDtypeStruct((keys, width), jnp.bfloat16),
            jax.ShapeDtypeStruct((keys, width), jnp.bfloat16),
        ),
        scratch_shapes=[
            pltpu.VMEM((keys // IMG_DEV, LANES), jnp.float32),
            pltpu.VMEM((keys // IMG_DEV, LANES), jnp.float32),
        ],
        compiler_params=pltpu.CompilerParams(vmem_limit_bytes=VMEM_LIMIT),
        cost_estimate=pl.CostEstimate(
            flops=28 * 10**9,
            bytes_accessed=keys * 3072,
            transcendentals=groups * rows * keys,
        ),
        name="cross_backward",
    )(split, queries, grads, stats, pairs, pairs)


def hidden_grads_kernel(rows_ref, grad_ref, gate_ref, up_ref, act_ref, out_ref):
    part = pl.program_id(0)
    source = (gate_ref, up_ref, act_ref)
    for index in range(3):

        @pl.when(part == index)
        def _():
            left = grad_ref if index == 2 else rows_ref
            out_ref[...] = mm(left[...], source[index][...], TN).astype(jnp.bfloat16)


def hidden_grads(rows, grads, gate, upward, act):
    row_count, width = rows.shape
    inner_width = gate.shape[1]
    blocks = lax.axis_size("head")
    block = inner_width // blocks
    whole = pl.BlockSpec((row_count, width), lambda p, j: (0, 0))

    def column(index):
        return pl.BlockSpec(
            (row_count, block), lambda p, j: (0, jnp.clip((p - index) * blocks + j, 0, blocks - 1))
        )

    return pl.pallas_call(
        hidden_grads_kernel,
        grid=(3, blocks),
        in_specs=[whole, whole, column(0), column(1), column(2)],
        out_specs=pl.BlockSpec((width, block), lambda p, j: (0, j * 3 + p)),
        out_shape=jax.ShapeDtypeStruct((width, 3 * inner_width), jnp.bfloat16),
        compiler_params=pltpu.CompilerParams(vmem_limit_bytes=VMEM_LIMIT),
        cost_estimate=pl.CostEstimate(
            flops=6 * row_count * width * inner_width,
            bytes_accessed=6 * width * inner_width,
            transcendentals=0,
        ),
        name="hidden_grads",
    )(rows, grads, gate, upward, act)


def rms_pull(values, gain, grad):
    inverse = lax.rsqrt(jnp.mean(values * values, axis=-1, keepdims=True) + norm_eps)
    hat = values * inverse
    scaled = grad * gain
    inner = jnp.mean(scaled * hat, axis=-1, keepdims=True)
    return inverse * (scaled - hat * inner), jnp.sum(grad * hat, axis=0)


def two_terms(values):
    high = lax.reduce_precision(values, exponent_bits=8, mantissa_bits=7)
    return high.astype(jnp.bfloat16), (values - high).astype(jnp.bfloat16)


def after(array, *earlier):
    marks = [e[(0,) * e.ndim].astype(jnp.float32) for e in earlier]
    mark = sum(marks[1:], marks[0])
    return jnp.where(mark == mark, array, jnp.asarray(jnp.nan, array.dtype))


def pick(array, index):
    return lax.dynamic_index_in_dim(array, index, 0, keepdims=False)


def send(array, bits, axis=("dp", "head")):
    dp_count = lax.axis_size("dp")
    head_count = lax.axis_size("head")
    dp_bits, head_bits = bits
    if head_bits == 0:
        return lax.ppermute(array, "dp", [(s, s ^ dp_bits) for s in range(dp_count)])
    if dp_bits == 0:
        return lax.ppermute(array, "head", [(s, s ^ head_bits) for s in range(head_count)])
    pairs = [
        (i * head_count + h, (i ^ dp_bits) * head_count + (h ^ head_bits))
        for i in range(dp_count)
        for h in range(head_count)
    ]
    return lax.ppermute(array, ("dp", "head"), pairs)


def in_order(pieces, index):
    bit = 1
    while bit < len(pieces):
        flip = (index & bit) != 0
        pieces = [jnp.where(flip, pieces[s ^ bit], pieces[s]) for s in range(len(pieces))]
        bit *= 2
    return pieces


def head_spread(block, far, late=None):
    head_count = lax.axis_size("head")
    head_index = lax.axis_index("head")
    held = jnp.stack(in_order([block, far], head_index // 2))
    came = send(held, (0, 1))
    came = came if late is None else after(came, late)
    lower, upper = in_order([held, came], head_index % 2)
    return [(lower, upper)[h % 2][h // 2] for h in range(head_count)]


def chip_pieces(blocks, chip):
    return [pick(blocks, chip)] + [
        send(pick(blocks, chip ^ d), (2 * d, 0)) for d in range(1, blocks.shape[0])
    ]


def chip_spread(block, chip):
    chips = lax.axis_size("dp") // 2
    return in_order([block] + [send(block, (2 * d, 0)) for d in range(1, chips)], chip)


def member_pieces(block_of):
    return [block_of(0)] + [send(block_of(d), (d & 1, d >> 1)) for d in range(1, 4)]


def head_halving(blocks):
    head_count = lax.axis_size("head")
    index = lax.axis_index("head")
    low, high = index % 2, index // 2
    by_low = blocks.reshape(head_count // 2, 2, *blocks.shape[1:])
    mine = lax.dynamic_index_in_dim(by_low, low, 1, keepdims=False)
    theirs = lax.dynamic_index_in_dim(by_low, 1 - low, 1, keepdims=False)
    both = mine.astype(jnp.float32) + send(theirs, (0, 1)).astype(jnp.float32)
    sent = both.astype(blocks.dtype)
    total = pick(both, high)
    for d in range(1, head_count // 2):
        total = total + send(pick(sent, high ^ d), (0, 2 * d)).astype(jnp.float32)
    return total


def all_sum(values):
    total = values + send(values, (1, 0))
    total = sum(chip_spread(total, lax.axis_index("dp") // 2))
    return sum(head_spread(total, send(total, (0, 2))))
def lamb_step(weight, grad, first, second, decay):
    mean = first_decay * first + (1.0 - first_decay) * grad
    square = second_decay * second + (1.0 - second_decay) * grad * grad
    step = (
        mean
        / (1.0 - first_decay**STEPS_DONE)
        / (jnp.sqrt(square / (1.0 - second_decay**STEPS_DONE)) + adam_eps)
        + decay * weight
    )
    return (mean, square, step)


def per_device(
    tokens,
    memory,
    cotangent,
    lengths,
    groups,
    image_map,
    entry_weights,
    exit_weights,
    expand_weights,
    contract_weights,
    norm_gains,
    entry_first,
    entry_second,
    exit_first,
    exit_second,
    expand_first,
    expand_second,
    contract_first,
    contract_second,
    gains_first,
    gains_second,
):
    dp_count = lax.axis_size("dp")
    head_count = lax.axis_size("head")
    dp_index = lax.axis_index("dp")
    head_index = lax.axis_index("head")
    chips = dp_count // 2
    chip, core = dp_index // 2, dp_index % 2
    side, near = head_index // 2, head_index % 2
    member = 2 * near + core
    here = core == side
    bf16 = jnp.bfloat16
    f32 = jnp.float32
    tok_rows, width = tokens.shape
    half_width = width // 2
    local = entry_weights.shape[2]
    hidden = expand_weights.shape[2]
    shard = width // dp_count
    row_count = tok_rows // 4
    image_count, patch_local = memory.shape[0:2]
    heads = local // HEAD_DIM

    def quarter(array):
        return pick(array.reshape(4, row_count, *array.shape[1:]), member)

    layout = jnp.stack([lengths, groups, image_map])
    layout = jnp.where(here, layout, send(layout, (1, 0)))
    stream_low = jnp.where(here, tokens, send(tokens, (1, 0)))
    other_rows = pick(cotangent.reshape(4, row_count, width), member ^ 1)
    cotangent_rows = jnp.where(here, quarter(cotangent), send(other_rows, (1, 0)))

    entry_low = entry_weights.astype(bf16).transpose(1, 0, 2)
    exit_low = exit_weights.astype(bf16).transpose(2, 0, 1)
    expand_low = expand_weights.astype(bf16).transpose(1, 0, 2)
    contract_low = contract_weights.astype(bf16).transpose(1, 0)[:, None]
    gains_low = jnp.pad(norm_gains.astype(bf16).transpose(1, 0), ((0, 0), (0, HEAD_DIM - 3)))

    def across(array):
        pairs = [
            (i * head_count + h, (i ^ 1) * head_count + (h ^ 2))
            for i in range(dp_count)
            for h in range(head_count)
            if i % 2 != h // 2
        ]
        return jnp.where(here, array, lax.ppermute(array, ("dp", "head"), pairs))

    moved = lax.all_to_all(
        memory.reshape(dp_count, IMG_DEV * patch_local, width),
        "dp",
        split_axis=0,
        concat_axis=0,
        tiled=True,
    )
    patches = dp_count * patch_local
    moved = moved.reshape(dp_count, IMG_DEV, patch_local, width).transpose(1, 0, 2, 3)
    moved = moved.reshape(IMG_DEV, patches, width)
    held = across(moved)
    other = send(held, (1, 0))
    memory_pair = jnp.concatenate([held, other], axis=1)
    memory_pair = memory_pair.reshape(2 * IMG_DEV * patches, width)

    own_set = entry_low[:, 0:3].reshape(shard, 3 * local)
    rest_set = jnp.concatenate([exit_low[:, 0:1], entry_low[:, 3:6], exit_low[:, 1:2]], axis=1)
    rest_set = rest_set.reshape(shard, 5 * local)
    far_set = send(jnp.concatenate([own_set, rest_set], axis=1), (0, 2))
    far_set = after(far_set, moved)
    far_set, far_rest = far_set[:, 0 : 3 * local], far_set[:, 3 * local :]
    mine = jnp.where(core == 0, own_set, far_set)
    theirs = jnp.where(core == 0, far_set, own_set)
    mine = jnp.concatenate([mine, gains_low], axis=1)
    theirs = send(jnp.concatenate([theirs, gains_low], axis=1), (1, 0))

    rest_set = jnp.stack(head_spread(rest_set, far_rest)).reshape(head_count, shard, 5, local)
    rest_set = rest_set.transpose(1, 2, 0, 3).reshape(shard, 5 * width)
    rest_full = lax.all_gather(rest_set, "dp", axis=0, tiled=True)
    exit_self_t = rest_full[:, 0:width]
    cross_query = rest_full[:, width : 2 * width]
    cross_pair = jnp.concatenate(
        [
            jnp.where(
                core == 0,
                rest_full[:, w * width : w * width + half_width],
                rest_full[:, w * width + half_width : (w + 1) * width],
            )
            for w in (2, 3)
        ],
        axis=1,
    )
    exit_cross_t = rest_full[:, 4 * width :]

    self_set = jnp.concatenate(in_order([mine, theirs], core), axis=0)
    self_full = [after(p, held) for p in chip_spread(self_set, chip)]
    self_full = jnp.concatenate(self_full, axis=0)
    gain_values = self_full[:, 3 * local : 3 * local + 3].astype(f32).transpose(1, 0)
    self_weights = jnp.concatenate(
        [
            jnp.pad(self_full[:, s * local : (s + 1) * local], ((0, 0), (0, 256 - local)))
            for s in range(3)
        ],
        axis=1,
    )

    segments, images, weights = token_layout(
        layout[0:1], layout[1:2], layout[2:3], tok_rows, IMG_DEV
    )
    image_tok = images[0]
    weight_tok = weights[0]
    text_ends = jnp.cumsum(layout[0])
    position = jnp.arange(tok_rows, dtype=jnp.int32)
    starts = jnp.max(
        jnp.where(position[None, :] >= text_ends[:, None], text_ends[:, None], 0), axis=0
    ).reshape(1, tok_rows)
    of_zero = (image_tok == 0).astype(jnp.int32)
    before = jnp.cumsum(of_zero)
    split = before[-1]
    place = jnp.where(image_tok == 0, before - 1, split + position - before)
    sorter = (place[None, :] == position[:, None]).astype(bf16)
    unsorter = (place[:, None] == position[None, :]).astype(bf16)
    split = split.reshape(1)

    stream = stream_low.astype(f32)
    hidden_one = rms_norm(stream, gain_values[0]).astype(bf16)
    qkv = mm(hidden_one, self_weights).astype(bf16)
    second_set = jnp.concatenate([expand_low, contract_low], axis=1)
    far_second = send(after(second_set, held), (0, 2))
    self_out, self_sums = self_forward(qkv, starts)
    columns = jnp.where(core == 0, head_index, head_index ^ 2)

    def by_member(array, d):
        return pick(array.reshape(4, row_count, *array.shape[1:]), member ^ d)

    self_block = self_out[:, 0:local]
    pieces = member_pieces(lambda d: by_member(self_block, d))
    far_second = after(far_second, self_block)
    pieces = in_order([pieces[0], pieces[2], pieces[1], pieces[3]], columns)
    self_rows = jnp.concatenate(pieces, axis=1)
    stream_rows = quarter(stream)
    stream_one = stream_rows + mm(self_rows, exit_self_t, NT)
    hidden_two = rms_norm(stream_one, gain_values[1]).astype(bf16)
    second_set = head_spread(second_set, far_second, stream_one)
    second_set = jnp.stack(second_set, axis=2).reshape(shard, 3 * head_count * hidden)
    second_full = lax.all_gather(second_set, "dp", axis=0, tiled=True)
    inner_width = head_count * hidden
    gate_weights = second_full[:, 0:inner_width]
    up_weights = second_full[:, inner_width : 2 * inner_width]
    contract_t = second_full[:, 2 * inner_width :]

    def by_core(array, d):
        flip = core == 1 - (d & 1)
        return jnp.where(flip, array[:, half_width:], array[:, 0:half_width])

    query_rows = mm(hidden_two, cross_query).astype(bf16)
    pieces = member_pieces(lambda d: by_core(query_rows, d))
    queries = mm(sorter, jnp.concatenate(in_order(pieces, member), axis=0)).astype(bf16)
    pairs = mm(memory_pair, cross_pair).astype(bf16)
    cross_out, cross_sums = cross_forward(split, queries, pairs)
    cross_out = mm(unsorter, cross_out).astype(bf16)
    high, low = two_terms(cross_sums[:, 0:2].reshape(2 * heads, tok_rows))
    tail = jnp.concatenate([high, low, jnp.zeros((4, tok_rows), bf16)], axis=0)
    tail = mm(tail, sorter).astype(bf16)
    tail = tail.reshape(16, 4, row_count).transpose(1, 0, 2)
    tail = jnp.pad(tail, ((0, 0), (0, 0), (0, half_width - row_count)))
    blocks = jnp.concatenate([cross_out.reshape(4, row_count, half_width), tail], axis=1)
    pieces = member_pieces(lambda d: pick(blocks, member ^ d))
    spread = (
        jnp.arange(2 * heads)[:, None] == (jnp.arange(half_width) // HEAD_DIM)[None, :]
    ).astype(f32)

    def lanes_of(per_head):
        return lax.dot_general(
            per_head, spread, TN, precision=lax.Precision.HIGHEST, preferred_element_type=f32
        )

    merged = []
    merged_sums = []
    for part in ([pieces[0], pieces[2]], [pieces[1], pieces[3]]):
        sums = [
            p[row_count : row_count + 2 * heads, 0:row_count].astype(f32)
            + p[row_count + 2 * heads : row_count + 4 * heads, 0:row_count].astype(f32)
            for p in part
        ]
        largest = jnp.maximum(sums[0], sums[1])
        both = [jnp.exp(s - largest) for s in sums]
        total = both[0] + both[1]
        merged.append(
            lanes_of(both[0] / total) * part[0][0:row_count].astype(f32)
            + lanes_of(both[1] / total) * part[1][0:row_count].astype(f32)
        )
        merged_sums.append(largest + jnp.log(total))
    cross_rows = jnp.concatenate(in_order(merged, core), axis=1).astype(bf16)
    stream_two = stream_one + mm(cross_rows, exit_cross_t, NT)
    hidden_three = rms_norm(stream_two, gain_values[2]).astype(bf16)

    gate = mm(hidden_three, gate_weights)
    upward = mm(hidden_three, up_weights)
    activated, pull_gate = jax.vjp(gated_hidden, gate, upward)
    activated_low = activated.astype(bf16)
    output_rows = stream_two + mm(activated_low, contract_t, NT)
    grad_rows = cotangent_rows.astype(f32) * quarter(weight_tok)[:, None]
    grad_low = grad_rows.astype(bf16)
    grad_gate, grad_up = pull_gate(mm(grad_low, contract_t))
    grad_gate = grad_gate.astype(bf16)
    grad_up = grad_up.astype(bf16)
    act_low = grad_low
    grad_normed = mm(grad_gate, gate_weights, NT) + mm(grad_up, up_weights, NT)
    grad_input, gain_three = rms_pull(stream_two, gain_values[2], grad_normed)
    grad_rows = grad_rows + grad_input
    def rows_within(rows):
        came = send(rows, (1, 0))
        return jnp.concatenate(in_order([rows, came], core), axis=0)

    def rows_across(rows):
        pairs = [
            (i * head_count + h, i * head_count + (h ^ 2))
            for i in range(dp_count)
            for h in range(head_count)
            if i % 2 == h // 2
        ]
        return jnp.where(here, rows, lax.ppermute(rows, ("dp", "head"), pairs))

    def rows_beside(rows):
        return jnp.concatenate(in_order([rows, send(rows, (0, 1))], near), axis=0)

    output = rows_across(rows_within(output_rows.astype(bf16)))

    grad_low = grad_rows.astype(bf16)
    exit_cross_part = mm(grad_low, cross_rows, TN).astype(bf16)
    grad_cross = mm(grad_low, exit_cross_t).astype(bf16)
    product = grad_cross.astype(f32) * cross_rows.astype(f32)
    tails = []
    for g in range(2):
        inner = lax.dot_general(
            spread,
            by_core(product, g),
            NT,
            precision=lax.Precision.HIGHEST,
            preferred_element_type=f32,
        )
        tail = jnp.concatenate([*two_terms(merged_sums[g]), *two_terms(inner)], axis=0)
        tails.append(jnp.pad(tail, ((0, 32 - 8 * heads), (0, half_width - row_count))))
    pieces = member_pieces(
        lambda d: jnp.concatenate([by_core(grad_cross, d), tails[d & 1]], axis=0)
    )
    second_part = hidden_grads(after(hidden_three, grad_cross), after(act_low, grad_cross), grad_gate, grad_up, activated_low)
    second_grads = lax.psum_scatter(second_part, "dp", scatter_dimension=0, tiled=True)
    got = after(jnp.stack(in_order(pieces, member)), second_part)
    grads = mm(sorter, got[:, 0:row_count].reshape(tok_rows, half_width)).astype(bf16)
    stats = (
        got[:, row_count : row_count + 8 * heads, 0:row_count]
        .transpose(1, 0, 2)
        .reshape(8 * heads, tok_rows)
    )
    stats = mm(stats, unsorter)
    sums = (stats[0 : 2 * heads] + stats[2 * heads : 4 * heads]).reshape(heads, 2, tok_rows)
    inner = (stats[4 * heads : 6 * heads] + stats[6 * heads :]).reshape(heads, 2, tok_rows)
    stats = jnp.concatenate([sums, inner, jnp.zeros((heads, 4, tok_rows), f32)], axis=1)
    grad_query, grad_key, grad_value = cross_backward(split, queries, grads, stats, pairs)
    grad_query = after(mm(unsorter, grad_query).astype(bf16), output)
    output = rows_beside(output).astype(f32)
    grad_pair = after(jnp.concatenate([grad_key, grad_value], axis=1), grad_query)
    memory_part = mm(grad_pair, cross_pair, NT).reshape(IMG_DEV, 2, patches, width)
    memory_came = send(memory_part[:, 1].astype(bf16), (1, 0))
    pair_part = mm(memory_pair, grad_pair, TN).astype(bf16)
    pieces = member_pieces(lambda d: by_member(grad_query, d))
    pieces = [p.astype(f32) for p in pieces]
    grad_query = jnp.concatenate(
        in_order([pieces[0] + pieces[2], pieces[1] + pieces[3]], core), axis=1
    ).astype(bf16)
    grad_input, gain_two = rms_pull(stream_one, gain_values[1], mm(grad_query, cross_query, NT))
    grad_rows = grad_rows + grad_input

    def core_halves(parts):
        parts = parts.reshape(-1, chips, 2, shard, width)
        kept = lax.dynamic_index_in_dim(parts, core, 2, keepdims=False)
        return kept, send(lax.dynamic_index_in_dim(parts, 1 - core, 2, keepdims=False), (1, 0))

    def chip_sum(parts):
        pieces = chip_pieces(parts.transpose(1, 0, 2, 3), chip)
        return sum(p.astype(f32) for p in pieces)

    query_part = mm(after(hidden_two, grad_rows), grad_query, TN).astype(bf16)
    kept, came = core_halves(jnp.stack([query_part, exit_cross_part]))
    pair_kept, pair_came = core_halves(pair_part)
    cross_sums = (kept.astype(f32) + came.astype(f32)).astype(bf16)
    cross_chips = jnp.concatenate([cross_sums, *in_order([pair_kept, pair_came], core)], axis=0)

    grad_low = grad_rows.astype(bf16)
    grad_self = mm(grad_low, exit_self_t).astype(bf16)
    grad_self = after(grad_self, output)
    by_columns = jnp.stack([grad_self[:, s * local : (s + 1) * local] for s in range(4)])
    pieces = member_pieces(lambda d: pick(by_columns, columns ^ (2 * (d & 1) + (d >> 1))))
    grad_self = jnp.pad(
        jnp.concatenate(in_order(pieces, member), axis=0), ((0, 0), (0, 256 - local))
    )
    grad_qkv = self_backward(qkv, grad_self, self_out, self_sums, starts)
    grad_normed = mm(grad_qkv, self_weights, NT)
    inverse = lax.rsqrt(jnp.mean(stream * stream, axis=-1, keepdims=True) + norm_eps)
    gain_one = jnp.sum(grad_normed * stream * inverse, axis=0)
    by_near = grad_normed.reshape(2, 2, row_count, width)
    kept = lax.dynamic_index_in_dim(by_near, core, 1, keepdims=False)
    came = lax.dynamic_index_in_dim(by_near, 1 - core, 1, keepdims=False).astype(bf16)
    self_core = mm(after(hidden_one, came), grad_qkv, TN).astype(bf16)
    kept = after(kept, self_core) + send(came, (1, 0)).astype(f32)
    came = send(pick(kept, 1 - near).astype(bf16), (0, 1))
    cross_chips = after(cross_chips, kept)
    cross_sums = chip_sum(cross_chips)
    memory_sum = after(memory_part[:, 0], cross_chips) + memory_came.astype(f32)
    memory_sum = memory_sum.astype(bf16)
    second_grads = after(second_grads, memory_sum)
    second_grads = jnp.concatenate(
        [second_grads[:, h * 3 * hidden : (h + 1) * 3 * hidden] for h in range(head_count)], axis=0
    )
    came = after(came, second_grads)
    memory_sum = across(memory_sum)
    second_grads = lax.psum_scatter(second_grads, "head", scatter_dimension=0, tiled=True)
    second_grads = second_grads.astype(f32)
    grad_normed = pick(kept, near) + came.astype(f32)
    grad_input, _ = rms_pull(stream_rows, gain_values[0], grad_normed)
    token_grads = (grad_rows + grad_input).astype(bf16)

    exit_self_part = mm(after(grad_low, token_grads), self_rows, TN).astype(bf16)
    kept, came = core_halves(exit_self_part)
    gain_part = jnp.stack([gain_one, gain_two, gain_three], axis=1).astype(bf16)
    gain_part = jnp.pad(gain_part, ((0, 0), (0, width - 3 * local - 3)))
    self_part = jnp.concatenate(
        [self_core[:, 256 * s : 256 * s + local] for s in range(3)] + [after(gain_part, token_grads)],
        axis=1,
    )
    self_part = self_part.reshape(chips, 2, shard, width)
    mine = lax.dynamic_index_in_dim(self_part, core, 1, keepdims=False)
    theirs = send(lax.dynamic_index_in_dim(self_part, 1 - core, 1, keepdims=False), (1, 0))
    token_grads = rows_within(token_grads)
    cross_sums = after(cross_sums, token_grads)
    token_grads = rows_across(token_grads)
    self_sums = jnp.stack(in_order([mine, theirs], core))
    self_sums = jnp.concatenate(
        [(kept.astype(f32) + came.astype(f32)).astype(bf16), self_sums], axis=0
    )
    self_sums = after(self_sums, cross_sums)
    token_grads = after(token_grads, self_sums, second_grads)
    self_sums = chip_sum(self_sums)

    sums = jnp.concatenate([self_sums[0:1], cross_sums, self_sums[1:3]], axis=0)
    sums = after(sums, token_grads, memory_sum)
    memory_grads = memory_sum.reshape(IMG_DEV, dp_count, patch_local, width).transpose(1, 0, 2, 3)
    memory_grads = lax.all_to_all(
        memory_grads.reshape(dp_count, IMG_DEV * patch_local, width),
        "dp",
        split_axis=0,
        concat_axis=0,
        tiled=True,
    )
    memory_grads = memory_grads.reshape(memory.shape).astype(f32)
    token_grads = rows_beside(token_grads).astype(f32)

    by_head = jnp.stack(
        [
            jnp.stack(
                [sums[w, :, h * local : (h + 1) * local] for w in range(3)]
                + [
                    sums[
                        3 + h // 2,
                        :,
                        w * half_width + (h % 2) * local : w * half_width + (h % 2 + 1) * local,
                    ]
                    for w in range(2)
                ]
                + [sums[5, :, 3 * local :] + sums[6, :, 3 * local :]]
            )
            for h in range(head_count)
        ]
    )
    by_head = by_head.reshape(2, 2, 6, shard, local)
    kept = lax.dynamic_index_in_dim(by_head, near, 1, keepdims=False)
    came = lax.dynamic_index_in_dim(by_head, 1 - near, 1, keepdims=False)
    kept = kept + send(came.astype(bf16), (0, 1)).astype(f32)
    own_three, far_three = [
        jnp.stack([sums[5 + w, :, s * local : (s + 1) * local] for s in range(3)]) for w in range(2)
    ]
    far_eight = jnp.concatenate([pick(kept, 1 - side), far_three], axis=0)
    own_eight = jnp.concatenate([pick(kept, side), own_three], axis=0)
    first_grads = own_eight + send(far_eight.astype(bf16), (0, 2)).astype(f32)
    exit_grads = jnp.stack([first_grads[0].T, first_grads[2].T])
    expand_grads = jnp.stack([second_grads[:, 0:hidden], second_grads[:, hidden : 2 * hidden]])
    contract_grads = second_grads[:, 2 * hidden :].T

    gain_grads = first_grads[5, :, 0:3].T
    entry_grads = jnp.stack([first_grads[w] for w in (6, 7, 8, 1, 3, 4)])

    entry_mean, entry_square, entry_step = lamb_step(
        entry_weights, entry_grads, entry_first, entry_second, weight_decay
    )
    exit_mean, exit_square, exit_step = lamb_step(
        exit_weights, exit_grads, exit_first, exit_second, weight_decay
    )
    expand_mean, expand_square, expand_step = lamb_step(
        expand_weights, expand_grads, expand_first, expand_second, weight_decay
    )
    contract_mean, contract_square, contract_step = lamb_step(
        contract_weights, contract_grads, contract_first, contract_second, weight_decay
    )
    gains_mean, gains_square, gains_step = lamb_step(
        norm_gains, gain_grads, gains_first, gains_second, 0.0
    )
    weight_local = jnp.concatenate(
        [
            jnp.sum(entry_weights * entry_weights, axis=(1, 2)),
            jnp.sum(exit_weights * exit_weights, axis=(1, 2)),
            jnp.sum(expand_weights * expand_weights, axis=(1, 2)),
            jnp.sum(contract_weights * contract_weights).reshape(1),
            jnp.sum(norm_gains * norm_gains, axis=1) / head_count,
        ]
    )
    step_local = jnp.concatenate(
        [
            jnp.sum(entry_step * entry_step, axis=(1, 2)),
            jnp.sum(exit_step * exit_step, axis=(1, 2)),
            jnp.sum(expand_step * expand_step, axis=(1, 2)),
            jnp.sum(contract_step * contract_step).reshape(1),
            jnp.sum(gains_step * gains_step, axis=1) / head_count,
        ]
    )
    weight_squares, step_squares = all_sum(after(jnp.stack([weight_local, step_local]), token_grads))
    weight_norm = jnp.sqrt(weight_squares)
    step_norm = jnp.sqrt(step_squares)
    ratio = learn_rate * weight_norm / (step_norm + adam_eps)
    entry_new = entry_weights - ratio[0:6][:, None, None] * entry_step
    exit_new = exit_weights - ratio[6:8][:, None, None] * exit_step
    expand_new = expand_weights - ratio[8:10][:, None, None] * expand_step
    contract_new = contract_weights - ratio[10] * contract_step
    gains_new = norm_gains - ratio[11:14][:, None] * gains_step
    trust_norms = jnp.stack([weight_norm, step_norm])
    return (
        output,
        token_grads,
        memory_grads,
        entry_grads,
        exit_grads,
        expand_grads,
        contract_grads,
        gain_grads,
        entry_mean,
        exit_mean,
        expand_mean,
        contract_mean,
        gains_mean,
        entry_square,
        exit_square,
        expand_square,
        contract_square,
        gains_square,
        entry_new,
        exit_new,
        expand_new,
        contract_new,
        gains_new,
        entry_new.astype(jnp.bfloat16),
        exit_new.astype(jnp.bfloat16),
        expand_new.astype(jnp.bfloat16),
        contract_new.astype(jnp.bfloat16),
        trust_norms,
    )


def solution(mesh):
    in_specs = (
        P("dp", None),
        P(None, ("dp", "head"), None),
        P("dp", None),
        P("dp"),
        P("dp"),
        P("dp"),
        P(None, "dp", "head"),
        P(None, "head", "dp"),
        P(None, "dp", "head"),
        P("head", "dp"),
        P(None, "dp"),
        P(None, "dp", "head"),
        P(None, "dp", "head"),
        P(None, "head", "dp"),
        P(None, "head", "dp"),
        P(None, "dp", "head"),
        P(None, "dp", "head"),
        P("head", "dp"),
        P("head", "dp"),
        P(None, "dp"),
        P(None, "dp"),
    )
    out_specs = (
        P("dp", None),
        P("dp", None),
        P(None, ("dp", "head"), None),
        P(None, "dp", "head"),
        P(None, "head", "dp"),
        P(None, "dp", "head"),
        P("head", "dp"),
        P(None, "dp"),
        P(None, "dp", "head"),
        P(None, "head", "dp"),
        P(None, "dp", "head"),
        P("head", "dp"),
        P(None, "dp"),
        P(None, "dp", "head"),
        P(None, "head", "dp"),
        P(None, "dp", "head"),
        P("head", "dp"),
        P(None, "dp"),
        P(None, "dp", "head"),
        P(None, "head", "dp"),
        P(None, "dp", "head"),
        P("head", "dp"),
        P(None, "dp"),
        P(None, "dp", "head"),
        P(None, "head", "dp"),
        P(None, "dp", "head"),
        P("head", "dp"),
        P(),
    )
    return jax.shard_map(
        per_device, mesh=mesh, in_specs=in_specs, out_specs=out_specs, check_vma=False
    )
```

```python
import jax
import jax.numpy as jnp
from jax import lax
from jax.experimental import pallas as pl
from jax.experimental.pallas import tpu as pltpu
from jax.sharding import PartitionSpec as P

HEAD_DIM = 64
IMG_DEV = 2
STEPS_DONE = 10


group_scale = (1.0, 0.5, 2.0)
first_decay = 0.9
second_decay = 0.999
learn_rate = 0.5
weight_decay = 0.01
adam_eps = 1e-06
norm_eps = 1e-06
masked_score = -1e30


def token_layout(lengths, groups, image_map, tok_rows, img_count):
    text_count = lengths.shape[1]
    text_ends = jnp.cumsum(lengths, axis=1)
    position = jnp.arange(tok_rows, dtype=jnp.int32)
    segment = jnp.sum((position[None, :, None] >= text_ends[:, None, :]).astype(jnp.int32), axis=2)
    chosen = (segment[:, :, None] == jnp.arange(text_count, dtype=jnp.int32)[None, None, :]).astype(
        jnp.int32
    )
    group_tok = jnp.sum(chosen * groups[:, None, :], axis=2)
    image_tok = jnp.sum(chosen * (image_map % img_count)[:, None, :], axis=2)
    scale_table = jnp.array(group_scale, dtype=jnp.float32)
    picked = (group_tok[:, :, None] == jnp.arange(3, dtype=jnp.int32)[None, None, :]).astype(
        jnp.float32
    )
    weight_tok = jnp.sum(picked * scale_table, axis=2) * (segment < text_count).astype(jnp.float32)
    return (segment, image_tok, weight_tok)


def rms_norm(values, gain):
    return values * lax.rsqrt(jnp.mean(values * values, axis=-1, keepdims=True) + norm_eps) * gain


def gated_hidden(gate, upward):
    return jax.nn.gelu(gate, approximate=True) * upward


BLOCK = 256
LANES = 128
LOG2E = 1.4426950408889634
NT = (((1,), (1,)), ((), ()))
TN = (((0,), (0,)), ((), ()))
VMEM_LIMIT = 50 * 1024 * 1024


def mm(a, b, dims=(((1,), (0,)), ((), ()))):
    return lax.dot_general(a, b, dims, preferred_element_type=jnp.float32)


def half_lanes(block, half):
    lane = lax.broadcasted_iota(jnp.int32, (1, LANES), 1)
    return jnp.where((lane // HEAD_DIM) == half, block, jnp.zeros_like(block))


def span_mask(start_ref, block, keys):
    low = block * BLOCK
    key_pos = lax.broadcasted_iota(jnp.int32, (keys, BLOCK), 0)
    query_pos = low + lax.broadcasted_iota(jnp.int32, (keys, BLOCK), 1)
    return (key_pos >= start_ref[0:1, low : low + BLOCK]) & (key_pos <= query_pos)


def self_forward_kernel(qkv_ref, start_ref, out_ref, sums_ref):
    rows = qkv_ref.shape[0]
    scale = HEAD_DIM ** (-0.5)
    sums_ref[...] = jnp.zeros_like(sums_ref)
    for pair in range(2):
        lanes = slice(LANES * pair, LANES * (pair + 1))
        for block in range(rows // BLOCK):
            own = slice(block * BLOCK, (block + 1) * BLOCK)
            keys = (block + 1) * BLOCK
            key_set = qkv_ref[0:keys, 256 + LANES * pair : 256 + LANES * (pair + 1)]
            value_set = qkv_ref[0:keys, 512 + LANES * pair : 512 + LANES * (pair + 1)]
            query_set = qkv_ref[own, lanes]
            allowed = span_mask(start_ref, block, keys)
            pieces = []
            for half in range(2 - pair):
                scores = mm(key_set, half_lanes(query_set, half), NT)
                scores = jnp.where(allowed, scores, masked_score)
                largest = jnp.max(scores, axis=0, keepdims=True)
                weights = jnp.exp2((scores - largest) * (scale * LOG2E))
                total = jnp.sum(weights, axis=0, keepdims=True)
                mixed = mm(value_set, weights.astype(jnp.bfloat16), TN) / total
                pieces.append(mixed[half * HEAD_DIM : (half + 1) * HEAD_DIM])
                row = 2 * pair + half
                sums_ref[row : row + 1, own] = largest * scale + jnp.log(total)
            if pair == 1:
                pieces.append(jnp.zeros_like(pieces[0]))
            out_ref[own, lanes] = jnp.concatenate(pieces, axis=0).T.astype(jnp.bfloat16)


def self_forward(qkv, starts):
    rows = qkv.shape[0]
    return pl.pallas_call(
        self_forward_kernel,
        out_shape=(
            jax.ShapeDtypeStruct((rows, 256), jnp.bfloat16),
            jax.ShapeDtypeStruct((8, rows), jnp.float32),
        ),
        compiler_params=pltpu.CompilerParams(vmem_limit_bytes=VMEM_LIMIT),
        cost_estimate=pl.CostEstimate(
            flops=6 * 10**9, bytes_accessed=rows * 2048, transcendentals=2 * rows * rows
        ),
        name="self_forward",
    )(qkv, starts)


def self_backward_kernel(
    qkv_ref, grad_ref, out_ref, sums_ref, start_ref, result_ref, key_acc, value_acc
):
    rows = qkv_ref.shape[0]
    scale = HEAD_DIM ** (-0.5)
    for pair in range(2):
        lanes = slice(LANES * pair, LANES * (pair + 1))
        key_lanes = slice(256 + LANES * pair, 256 + LANES * (pair + 1))
        value_lanes = slice(512 + LANES * pair, 512 + LANES * (pair + 1))
        for block in reversed(range(rows // BLOCK)):
            own = slice(block * BLOCK, (block + 1) * BLOCK)
            keys = (block + 1) * BLOCK
            key_set = qkv_ref[0:keys, key_lanes]
            value_set = qkv_ref[0:keys, value_lanes]
            query_set = qkv_ref[own, lanes]
            grad_set = grad_ref[own, lanes]
            allowed = span_mask(start_ref, block, keys)
            product = (
                grad_set.astype(jnp.float32) * out_ref[own, lanes].astype(jnp.float32)
            ).T
            pieces = []
            key_part = None
            for half in range(2 - pair):
                row = 2 * pair + half
                inner = jnp.sum(
                    product[half * HEAD_DIM : (half + 1) * HEAD_DIM], axis=0, keepdims=True
                )
                query_half = half_lanes(query_set, half)
                grad_half = half_lanes(grad_set, half)
                scores = mm(key_set, query_half, NT)
                probs = jnp.where(
                    allowed,
                    jnp.exp2(scores * (scale * LOG2E) - sums_ref[row : row + 1, own] * LOG2E),
                    0.0,
                )
                grad_probs = mm(value_set, grad_half, NT)
                grad_scores = (probs * (grad_probs - inner)).astype(jnp.bfloat16)
                value_new = mm(probs.astype(jnp.bfloat16), grad_half)
                key_new = mm(grad_scores, query_half)
                key_part = key_new if key_part is None else key_part + key_new
                value_part = value_new if half == 0 else value_part + value_new
                mixed = mm(key_set, grad_scores, TN) * scale
                pieces.append(mixed[half * HEAD_DIM : (half + 1) * HEAD_DIM])
            if pair == 1:
                pieces.append(jnp.zeros_like(pieces[0]))
            result_ref[own, lanes] = jnp.concatenate(pieces, axis=0).T.astype(jnp.bfloat16)
            if keys == rows:
                key_acc[...] = key_part
                value_acc[...] = value_part
            else:
                key_acc[0:keys, :] += key_part
                value_acc[0:keys, :] += value_part
        result_ref[:, key_lanes] = (key_acc[...] * scale).astype(jnp.bfloat16)
        result_ref[:, value_lanes] = value_acc[...].astype(jnp.bfloat16)


def self_backward(qkv, grad_out, out, sums, starts):
    rows = qkv.shape[0]
    return pl.pallas_call(
        self_backward_kernel,
        out_shape=jax.ShapeDtypeStruct((rows, 768), jnp.bfloat16),
        scratch_shapes=[
            pltpu.VMEM((rows, LANES), jnp.float32),
            pltpu.VMEM((rows, LANES), jnp.float32),
        ],
        compiler_params=pltpu.CompilerParams(vmem_limit_bytes=VMEM_LIMIT),
        cost_estimate=pl.CostEstimate(
            flops=8 * 10**9, bytes_accessed=rows * 5120, transcendentals=2 * rows * rows
        ),
        name="self_backward",
    )(qkv, grad_out, out, sums, starts)


def image_blocks(split, image, blocks):
    if image == 0:
        return 0, (split + BLOCK - 1) // BLOCK
    return split // BLOCK, blocks


def own_columns(split, image, low):
    column = low + lax.broadcasted_iota(jnp.int32, (1, BLOCK), 1)
    return column < split if image == 0 else column >= split


def own_rows(split, image, low):
    row = low + lax.broadcasted_iota(jnp.int32, (BLOCK, LANES), 0)
    return row < split if image == 0 else row >= split


def cross_forward_kernel(split_ref, query_ref, key_ref, value_ref, out_ref, sums_ref):
    rows = query_ref.shape[0]
    keys = key_ref.shape[0] // IMG_DEV
    scale = HEAD_DIM ** (-0.5)
    split = split_ref[0]
    for image in range(IMG_DEV):
        first, last = image_blocks(split, image, rows // BLOCK)

        def step(block, carry):
            low = pl.multiple_of(block * BLOCK, BLOCK)
            query_set = query_ref[pl.ds(low, BLOCK), :]
            key_set = key_ref[image * keys : (image + 1) * keys, :]
            value_set = value_ref[image * keys : (image + 1) * keys, :]
            kept = own_columns(split, image, low)
            halves = jnp.concatenate([half_lanes(query_set, half) for half in range(2)], axis=0)
            scores = mm(key_set, halves, NT)
            largest = jnp.max(scores, axis=0, keepdims=True)
            weights = jnp.exp2((scores - largest) * (scale * LOG2E))
            total = jnp.sum(weights, axis=0, keepdims=True)
            mixed = mm(value_set, weights.astype(jnp.bfloat16), TN) / total
            logs = largest * scale + jnp.log(total)
            pieces = []
            for half in range(2):
                own = slice(half * BLOCK, (half + 1) * BLOCK)
                pieces.append(mixed[half * HEAD_DIM : (half + 1) * HEAD_DIM, own])
                held = sums_ref[0, half : half + 1, pl.ds(low, BLOCK)]
                sums_ref[0, half : half + 1, pl.ds(low, BLOCK)] = jnp.where(
                    kept, logs[:, own], held
                )
            fresh = jnp.concatenate(pieces, axis=0).T
            held = out_ref[pl.ds(low, BLOCK), :].astype(jnp.float32)
            out_ref[pl.ds(low, BLOCK), :] = jnp.where(
                own_rows(split, image, low), fresh, held
            ).astype(jnp.bfloat16)
            return carry

        lax.fori_loop(first, last, step, 0)


def cross_forward(split, queries, pairs):
    rows, width = queries.shape
    keys = pairs.shape[0]
    groups = width // LANES
    return pl.pallas_call(
        cross_forward_kernel,
        grid=(groups,),
        in_specs=[
            pl.BlockSpec(memory_space=pltpu.SMEM),
            pl.BlockSpec((rows, LANES), lambda j: (0, j)),
            pl.BlockSpec((keys, LANES), lambda j: (0, j)),
            pl.BlockSpec((keys, LANES), lambda j: (0, groups + j)),
        ],
        out_specs=(
            pl.BlockSpec((rows, LANES), lambda j: (0, j)),
            pl.BlockSpec((1, 8, rows), lambda j: (j, 0, 0)),
        ),
        out_shape=(
            jax.ShapeDtypeStruct((rows, width), jnp.bfloat16),
            jax.ShapeDtypeStruct((groups, 8, rows), jnp.float32),
        ),
        compiler_params=pltpu.CompilerParams(vmem_limit_bytes=VMEM_LIMIT),
        cost_estimate=pl.CostEstimate(
            flops=28 * 10**9,
            bytes_accessed=keys * 1536,
            transcendentals=groups * rows * keys,
        ),
        name="cross_forward",
    )(split, queries, pairs, pairs)


def cross_backward_kernel(
    split_ref,
    query_ref,
    grad_ref,
    stats_ref,
    key_ref,
    value_ref,
    query_out,
    key_out,
    value_out,
    key_acc,
    value_acc,
):
    rows = query_ref.shape[0]
    keys = key_ref.shape[0] // IMG_DEV
    scale = HEAD_DIM ** (-0.5)
    split = split_ref[0]
    for image in range(IMG_DEV):
        first, last = image_blocks(split, image, rows // BLOCK)
        span = slice(image * keys, (image + 1) * keys)
        key_acc[...] = jnp.zeros_like(key_acc)
        value_acc[...] = jnp.zeros_like(value_acc)

        def step(block, carry):
            low = pl.multiple_of(block * BLOCK, BLOCK)
            query_set = query_ref[pl.ds(low, BLOCK), :]
            grad_set = grad_ref[pl.ds(low, BLOCK), :]
            key_set = key_ref[span, :]
            value_set = value_ref[span, :]
            kept = own_columns(split, image, low)
            shifts, inners = [], []
            for half in range(2):
                sums = stats_ref[0, half : half + 1, pl.ds(low, BLOCK)]
                inners.append(stats_ref[0, 2 + half : 3 + half, pl.ds(low, BLOCK)])
                shifts.append(jnp.where(kept, sums * LOG2E, -masked_score))
            shift = jnp.concatenate(shifts, axis=1)
            inner = jnp.concatenate(inners, axis=1)
            queries = jnp.concatenate([half_lanes(query_set, half) for half in range(2)], axis=0)
            grads = jnp.concatenate([half_lanes(grad_set, half) for half in range(2)], axis=0)
            scores = mm(key_set, queries, NT)
            probs = jnp.exp2(scores * (scale * LOG2E) - shift)
            grad_probs = mm(value_set, grads, NT)
            grad_scores = (probs * (grad_probs - inner)).astype(jnp.bfloat16)
            value_acc[...] += mm(probs.astype(jnp.bfloat16), grads)
            key_acc[...] += mm(grad_scores, queries)
            mixed = mm(key_set, grad_scores, TN) * scale
            pieces = [
                mixed[half * HEAD_DIM : (half + 1) * HEAD_DIM, half * BLOCK : (half + 1) * BLOCK]
                for half in range(2)
            ]
            fresh = jnp.concatenate(pieces, axis=0).T
            held = query_out[pl.ds(low, BLOCK), :].astype(jnp.float32)
            query_out[pl.ds(low, BLOCK), :] = jnp.where(
                own_rows(split, image, low), fresh, held
            ).astype(jnp.bfloat16)
            return carry

        lax.fori_loop(first, last, step, 0)
        key_out[span, :] = (key_acc[...] * scale).astype(jnp.bfloat16)
        value_out[span, :] = value_acc[...].astype(jnp.bfloat16)


def cross_backward(split, queries, grads, stats, pairs):
    rows, width = queries.shape
    keys = pairs.shape[0]
    groups = width // LANES
    return pl.pallas_call(
        cross_backward_kernel,
        grid=(groups,),
        in_specs=[
            pl.BlockSpec(memory_space=pltpu.SMEM),
            pl.BlockSpec((rows, LANES), lambda j: (0, j)),
            pl.BlockSpec((rows, LANES), lambda j: (0, j)),
            pl.BlockSpec((1, 8, rows), lambda j: (j, 0, 0)),
            pl.BlockSpec((keys, LANES), lambda j: (0, j)),
            pl.BlockSpec((keys, LANES), lambda j: (0, groups + j)),
        ],
        out_specs=(
            pl.BlockSpec((rows, LANES), lambda j: (0, j)),
            pl.BlockSpec((keys, LANES), lambda j: (0, j)),
            pl.BlockSpec((keys, LANES), lambda j: (0, j)),
        ),
        out_shape=(
            jax.ShapeDtypeStruct((rows, width), jnp.bfloat16),
            jax.ShapeDtypeStruct((keys, width), jnp.bfloat16),
            jax.ShapeDtypeStruct((keys, width), jnp.bfloat16),
        ),
        scratch_shapes=[
            pltpu.VMEM((keys // IMG_DEV, LANES), jnp.float32),
            pltpu.VMEM((keys // IMG_DEV, LANES), jnp.float32),
        ],
        compiler_params=pltpu.CompilerParams(vmem_limit_bytes=VMEM_LIMIT),
        cost_estimate=pl.CostEstimate(
            flops=28 * 10**9,
            bytes_accessed=keys * 3072,
            transcendentals=groups * rows * keys,
        ),
        name="cross_backward",
    )(split, queries, grads, stats, pairs, pairs)


def hidden_grads_kernel(rows_ref, grad_ref, gate_ref, up_ref, act_ref, out_ref):
    part = pl.program_id(0)
    source = (gate_ref, up_ref, act_ref)
    for index in range(3):

        @pl.when(part == index)
        def _():
            left = grad_ref if index == 2 else rows_ref
            out_ref[...] = mm(left[...], source[index][...], TN).astype(jnp.bfloat16)


def hidden_grads(rows, grads, gate, upward, act):
    row_count, width = rows.shape
    inner_width = gate.shape[1]
    blocks = lax.axis_size("head")
    block = inner_width // blocks
    whole = pl.BlockSpec((row_count, width), lambda p, j: (0, 0))

    def column(index):
        return pl.BlockSpec(
            (row_count, block), lambda p, j: (0, jnp.clip((p - index) * blocks + j, 0, blocks - 1))
        )

    return pl.pallas_call(
        hidden_grads_kernel,
        grid=(3, blocks),
        in_specs=[whole, whole, column(0), column(1), column(2)],
        out_specs=pl.BlockSpec((width, block), lambda p, j: (0, j * 3 + p)),
        out_shape=jax.ShapeDtypeStruct((width, 3 * inner_width), jnp.bfloat16),
        compiler_params=pltpu.CompilerParams(vmem_limit_bytes=VMEM_LIMIT),
        cost_estimate=pl.CostEstimate(
            flops=6 * row_count * width * inner_width,
            bytes_accessed=6 * width * inner_width,
            transcendentals=0,
        ),
        name="hidden_grads",
    )(rows, grads, gate, upward, act)


def rms_pull(values, gain, grad):
    inverse = lax.rsqrt(jnp.mean(values * values, axis=-1, keepdims=True) + norm_eps)
    hat = values * inverse
    scaled = grad * gain
    inner = jnp.mean(scaled * hat, axis=-1, keepdims=True)
    return inverse * (scaled - hat * inner), jnp.sum(grad * hat, axis=0)


def two_terms(values):
    high = lax.reduce_precision(values, exponent_bits=8, mantissa_bits=7)
    return high.astype(jnp.bfloat16), (values - high).astype(jnp.bfloat16)


def after(array, *earlier):
    marks = [e[(0,) * e.ndim].astype(jnp.float32) for e in earlier]
    mark = sum(marks[1:], marks[0])
    return jnp.where(mark == mark, array, jnp.asarray(jnp.nan, array.dtype))


def pick(array, index):
    return lax.dynamic_index_in_dim(array, index, 0, keepdims=False)


def send(array, bits, axis=("dp", "head")):
    dp_count = lax.axis_size("dp")
    head_count = lax.axis_size("head")
    dp_bits, head_bits = bits
    if head_bits == 0:
        return lax.ppermute(array, "dp", [(s, s ^ dp_bits) for s in range(dp_count)])
    if dp_bits == 0:
        return lax.ppermute(array, "head", [(s, s ^ head_bits) for s in range(head_count)])
    pairs = [
        (i * head_count + h, (i ^ dp_bits) * head_count + (h ^ head_bits))
        for i in range(dp_count)
        for h in range(head_count)
    ]
    return lax.ppermute(array, ("dp", "head"), pairs)


def in_order(pieces, index):
    bit = 1
    while bit < len(pieces):
        flip = (index & bit) != 0
        pieces = [jnp.where(flip, pieces[s ^ bit], pieces[s]) for s in range(len(pieces))]
        bit *= 2
    return pieces


def head_spread(block, far, late=None):
    head_count = lax.axis_size("head")
    head_index = lax.axis_index("head")
    held = jnp.stack(in_order([block, far], head_index // 2))
    came = send(held, (0, 1))
    came = came if late is None else after(came, late)
    lower, upper = in_order([held, came], head_index % 2)
    return [(lower, upper)[h % 2][h // 2] for h in range(head_count)]


def chip_pieces(blocks, chip):
    return [pick(blocks, chip)] + [
        send(pick(blocks, chip ^ d), (2 * d, 0)) for d in range(1, blocks.shape[0])
    ]


def chip_spread(block, chip):
    chips = lax.axis_size("dp") // 2
    return in_order([block] + [send(block, (2 * d, 0)) for d in range(1, chips)], chip)


def member_pieces(block_of):
    return [block_of(0)] + [send(block_of(d), (d & 1, d >> 1)) for d in range(1, 4)]


def head_halving(blocks):
    head_count = lax.axis_size("head")
    index = lax.axis_index("head")
    low, high = index % 2, index // 2
    by_low = blocks.reshape(head_count // 2, 2, *blocks.shape[1:])
    mine = lax.dynamic_index_in_dim(by_low, low, 1, keepdims=False)
    theirs = lax.dynamic_index_in_dim(by_low, 1 - low, 1, keepdims=False)
    both = mine.astype(jnp.float32) + send(theirs, (0, 1)).astype(jnp.float32)
    sent = both.astype(blocks.dtype)
    total = pick(both, high)
    for d in range(1, head_count // 2):
        total = total + send(pick(sent, high ^ d), (0, 2 * d)).astype(jnp.float32)
    return total


def all_sum(values):
    total = values + send(values, (1, 0))
    total = sum(chip_spread(total, lax.axis_index("dp") // 2))
    return sum(head_spread(total, send(total, (0, 2))))
def lamb_step(weight, grad, first, second, decay):
    mean = first_decay * first + (1.0 - first_decay) * grad
    square = second_decay * second + (1.0 - second_decay) * grad * grad
    step = (
        mean
        / (1.0 - first_decay**STEPS_DONE)
        / (jnp.sqrt(square / (1.0 - second_decay**STEPS_DONE)) + adam_eps)
        + decay * weight
    )
    return (mean, square, step)


def per_device(
    tokens,
    memory,
    cotangent,
    lengths,
    groups,
    image_map,
    entry_weights,
    exit_weights,
    expand_weights,
    contract_weights,
    norm_gains,
    entry_first,
    entry_second,
    exit_first,
    exit_second,
    expand_first,
    expand_second,
    contract_first,
    contract_second,
    gains_first,
    gains_second,
):
    dp_count = lax.axis_size("dp")
    head_count = lax.axis_size("head")
    dp_index = lax.axis_index("dp")
    head_index = lax.axis_index("head")
    chips = dp_count // 2
    chip, core = dp_index // 2, dp_index % 2
    side, near = head_index // 2, head_index % 2
    member = 2 * near + core
    here = core == side
    bf16 = jnp.bfloat16
    f32 = jnp.float32
    tok_rows, width = tokens.shape
    half_width = width // 2
    local = entry_weights.shape[2]
    hidden = expand_weights.shape[2]
    shard = width // dp_count
    row_count = tok_rows // 4
    image_count, patch_local = memory.shape[0:2]
    heads = local // HEAD_DIM

    def quarter(array):
        return pick(array.reshape(4, row_count, *array.shape[1:]), member)

    layout = jnp.stack([lengths, groups, image_map])
    layout = jnp.where(here, layout, send(layout, (1, 0)))
    stream_low = jnp.where(here, tokens, send(tokens, (1, 0)))
    other_rows = pick(cotangent.reshape(4, row_count, width), member ^ 1)
    cotangent_rows = jnp.where(here, quarter(cotangent), send(other_rows, (1, 0)))

    segments, images, weights = token_layout(
        layout[0:1], layout[1:2], layout[2:3], tok_rows, IMG_DEV
    )
    image_tok = images[0]
    weight_tok = weights[0]
    text_ends = jnp.cumsum(layout[0])
    position = jnp.arange(tok_rows, dtype=jnp.int32)
    starts = jnp.max(
        jnp.where(position[None, :] >= text_ends[:, None], text_ends[:, None], 0), axis=0
    ).reshape(1, tok_rows)
    of_zero = (image_tok == 0).astype(jnp.int32)
    before = jnp.cumsum(of_zero)
    split = before[-1]
    place = jnp.where(image_tok == 0, before - 1, split + position - before)
    sorter = (place[None, :] == position[:, None]).astype(bf16)
    unsorter = (place[:, None] == position[None, :]).astype(bf16)
    split = split.reshape(1)

    entry_low = entry_weights.astype(bf16).transpose(1, 0, 2)
    exit_low = exit_weights.astype(bf16).transpose(2, 0, 1)
    expand_low = expand_weights.astype(bf16).transpose(1, 0, 2)
    contract_low = contract_weights.astype(bf16).transpose(1, 0)[:, None]
    gains_low = jnp.pad(norm_gains.astype(bf16).transpose(1, 0), ((0, 0), (0, HEAD_DIM - 3)))

    def across(array):
        pairs = [
            (i * head_count + h, (i ^ 1) * head_count + (h ^ 2))
            for i in range(dp_count)
            for h in range(head_count)
            if i % 2 != h // 2
        ]
        return jnp.where(here, array, lax.ppermute(array, ("dp", "head"), pairs))

    moved = lax.all_to_all(
        memory.reshape(dp_count, IMG_DEV * patch_local, width),
        "dp",
        split_axis=0,
        concat_axis=0,
        tiled=True,
    )
    patches = dp_count * patch_local
    moved = moved.reshape(dp_count, IMG_DEV, patch_local, width).transpose(1, 0, 2, 3)
    moved = moved.reshape(IMG_DEV, patches, width)
    held = across(moved)
    other = send(held, (1, 0))
    memory_pair = jnp.concatenate([held, other], axis=1)
    memory_pair = memory_pair.reshape(2 * IMG_DEV * patches, width)

    own_set = entry_low[:, 0:3].reshape(shard, 3 * local)
    rest_set = jnp.concatenate([exit_low[:, 0:1], entry_low[:, 3:6], exit_low[:, 1:2]], axis=1)
    rest_set = rest_set.reshape(shard, 5 * local)
    far_set = send(jnp.concatenate([own_set, rest_set], axis=1), (0, 2))
    far_set = after(far_set, moved)
    far_set, far_rest = far_set[:, 0 : 3 * local], far_set[:, 3 * local :]
    mine = jnp.where(core == 0, own_set, far_set)
    theirs = jnp.where(core == 0, far_set, own_set)
    mine = jnp.concatenate([mine, gains_low], axis=1)
    theirs = send(jnp.concatenate([theirs, gains_low], axis=1), (1, 0))

    rest_set = jnp.stack(head_spread(rest_set, far_rest)).reshape(head_count, shard, 5, local)
    rest_set = rest_set.transpose(1, 2, 0, 3).reshape(shard, 5 * width)
    rest_full = lax.all_gather(rest_set, "dp", axis=0, tiled=True)
    exit_self_t = rest_full[:, 0:width]
    cross_query = rest_full[:, width : 2 * width]
    cross_pair = jnp.concatenate(
        [
            jnp.where(
                core == 0,
                rest_full[:, w * width : w * width + half_width],
                rest_full[:, w * width + half_width : (w + 1) * width],
            )
            for w in (2, 3)
        ],
        axis=1,
    )
    exit_cross_t = rest_full[:, 4 * width :]

    self_set = jnp.concatenate(in_order([mine, theirs], core), axis=0)
    self_set = after(self_set, place, weight_tok, starts)
    self_full = [after(p, held) for p in chip_spread(self_set, chip)]
    self_full = jnp.concatenate(self_full, axis=0)
    gain_values = self_full[:, 3 * local : 3 * local + 3].astype(f32).transpose(1, 0)
    self_weights = jnp.concatenate(
        [
            jnp.pad(self_full[:, s * local : (s + 1) * local], ((0, 0), (0, 256 - local)))
            for s in range(3)
        ],
        axis=1,
    )

    stream = stream_low.astype(f32)
    hidden_one = rms_norm(stream, gain_values[0]).astype(bf16)
    qkv = mm(hidden_one, self_weights).astype(bf16)
    second_set = jnp.concatenate([expand_low, contract_low], axis=1)
    far_second = send(after(second_set, held), (0, 2))
    self_out, self_sums = self_forward(qkv, starts)
    columns = jnp.where(core == 0, head_index, head_index ^ 2)

    def by_member(array, d):
        return pick(array.reshape(4, row_count, *array.shape[1:]), member ^ d)

    self_block = self_out[:, 0:local]
    pieces = member_pieces(lambda d: by_member(self_block, d))
    far_second = after(far_second, self_block)
    pieces = in_order([pieces[0], pieces[2], pieces[1], pieces[3]], columns)
    self_rows = jnp.concatenate(pieces, axis=1)
    stream_rows = quarter(stream)
    stream_one = stream_rows + mm(self_rows, exit_self_t, NT)
    hidden_two = rms_norm(stream_one, gain_values[1]).astype(bf16)
    second_set = head_spread(second_set, far_second, stream_one)
    second_set = jnp.stack(second_set, axis=2).reshape(shard, 3 * head_count * hidden)
    second_full = lax.all_gather(second_set, "dp", axis=0, tiled=True)
    inner_width = head_count * hidden
    gate_weights = second_full[:, 0:inner_width]
    up_weights = second_full[:, inner_width : 2 * inner_width]
    contract_t = second_full[:, 2 * inner_width :]

    def by_core(array, d):
        flip = core == 1 - (d & 1)
        return jnp.where(flip, array[:, half_width:], array[:, 0:half_width])

    query_rows = mm(hidden_two, cross_query).astype(bf16)
    pieces = member_pieces(lambda d: by_core(query_rows, d))
    queries = mm(sorter, jnp.concatenate(in_order(pieces, member), axis=0)).astype(bf16)
    pairs = mm(memory_pair, cross_pair).astype(bf16)
    cross_out, cross_sums = cross_forward(split, queries, pairs)
    cross_out = mm(unsorter, cross_out).astype(bf16)
    high, low = two_terms(cross_sums[:, 0:2].reshape(2 * heads, tok_rows))
    tail = jnp.concatenate([high, low, jnp.zeros((4, tok_rows), bf16)], axis=0)
    tail = mm(tail, sorter).astype(bf16)
    tail = tail.reshape(16, 4, row_count).transpose(1, 0, 2)
    tail = jnp.pad(tail, ((0, 0), (0, 0), (0, half_width - row_count)))
    blocks = jnp.concatenate([cross_out.reshape(4, row_count, half_width), tail], axis=1)
    pieces = member_pieces(lambda d: pick(blocks, member ^ d))
    spread = (
        jnp.arange(2 * heads)[:, None] == (jnp.arange(half_width) // HEAD_DIM)[None, :]
    ).astype(f32)

    def lanes_of(per_head):
        return lax.dot_general(
            per_head, spread, TN, precision=lax.Precision.HIGHEST, preferred_element_type=f32
        )

    merged = []
    merged_sums = []
    for part in ([pieces[0], pieces[2]], [pieces[1], pieces[3]]):
        sums = [
            p[row_count : row_count + 2 * heads, 0:row_count].astype(f32)
            + p[row_count + 2 * heads : row_count + 4 * heads, 0:row_count].astype(f32)
            for p in part
        ]
        largest = jnp.maximum(sums[0], sums[1])
        both = [jnp.exp(s - largest) for s in sums]
        total = both[0] + both[1]
        merged.append(
            lanes_of(both[0] / total) * part[0][0:row_count].astype(f32)
            + lanes_of(both[1] / total) * part[1][0:row_count].astype(f32)
        )
        merged_sums.append(largest + jnp.log(total))
    cross_rows = jnp.concatenate(in_order(merged, core), axis=1).astype(bf16)
    stream_two = stream_one + mm(cross_rows, exit_cross_t, NT)
    hidden_three = rms_norm(stream_two, gain_values[2]).astype(bf16)

    gate = mm(hidden_three, gate_weights)
    upward = mm(hidden_three, up_weights)
    activated, pull_gate = jax.vjp(gated_hidden, gate, upward)
    activated_low = activated.astype(bf16)
    output_rows = stream_two + mm(activated_low, contract_t, NT)
    grad_rows = cotangent_rows.astype(f32) * quarter(weight_tok)[:, None]
    grad_low = grad_rows.astype(bf16)
    grad_gate, grad_up = pull_gate(mm(grad_low, contract_t))
    grad_gate = grad_gate.astype(bf16)
    grad_up = grad_up.astype(bf16)
    act_low = grad_low
    grad_normed = mm(grad_gate, gate_weights, NT) + mm(grad_up, up_weights, NT)
    grad_input, gain_three = rms_pull(stream_two, gain_values[2], grad_normed)
    grad_rows = grad_rows + grad_input
    def rows_within(rows):
        came = send(rows, (1, 0))
        return jnp.concatenate(in_order([rows, came], core), axis=0)

    def rows_across(rows):
        pairs = [
            (i * head_count + h, i * head_count + (h ^ 2))
            for i in range(dp_count)
            for h in range(head_count)
            if i % 2 == h // 2
        ]
        return jnp.where(here, rows, lax.ppermute(rows, ("dp", "head"), pairs))

    def rows_beside(rows):
        return jnp.concatenate(in_order([rows, send(rows, (0, 1))], near), axis=0)

    output = rows_across(rows_within(output_rows.astype(bf16)))

    grad_low = grad_rows.astype(bf16)
    exit_cross_part = mm(grad_low, cross_rows, TN).astype(bf16)
    grad_cross = mm(grad_low, exit_cross_t).astype(bf16)
    product = grad_cross.astype(f32) * cross_rows.astype(f32)
    tails = []
    for g in range(2):
        inner = lax.dot_general(
            spread,
            by_core(product, g),
            NT,
            precision=lax.Precision.HIGHEST,
            preferred_element_type=f32,
        )
        tail = jnp.concatenate([*two_terms(merged_sums[g]), *two_terms(inner)], axis=0)
        tails.append(jnp.pad(tail, ((0, 32 - 8 * heads), (0, half_width - row_count))))
    pieces = member_pieces(
        lambda d: jnp.concatenate([by_core(grad_cross, d), tails[d & 1]], axis=0)
    )
    second_part = hidden_grads(after(hidden_three, grad_cross), after(act_low, grad_cross), grad_gate, grad_up, activated_low)
    second_grads = lax.psum_scatter(second_part, "dp", scatter_dimension=0, tiled=True)
    got = after(jnp.stack(in_order(pieces, member)), second_part)
    grads = mm(sorter, got[:, 0:row_count].reshape(tok_rows, half_width)).astype(bf16)
    stats = (
        got[:, row_count : row_count + 8 * heads, 0:row_count]
        .transpose(1, 0, 2)
        .reshape(8 * heads, tok_rows)
    )
    stats = mm(stats, unsorter)
    sums = (stats[0 : 2 * heads] + stats[2 * heads : 4 * heads]).reshape(heads, 2, tok_rows)
    inner = (stats[4 * heads : 6 * heads] + stats[6 * heads :]).reshape(heads, 2, tok_rows)
    stats = jnp.concatenate([sums, inner, jnp.zeros((heads, 4, tok_rows), f32)], axis=1)
    grad_query, grad_key, grad_value = cross_backward(split, queries, grads, stats, pairs)
    grad_query = after(mm(unsorter, grad_query).astype(bf16), output)
    grad_pair = after(jnp.concatenate([grad_key, grad_value], axis=1), grad_query)
    memory_part = mm(grad_pair, cross_pair, NT).reshape(IMG_DEV, 2, patches, width)
    memory_came = send(memory_part[:, 1].astype(bf16), (1, 0))
    pair_part = mm(memory_pair, grad_pair, TN).astype(bf16)
    pieces = member_pieces(lambda d: by_member(grad_query, d))
    pieces = [p.astype(f32) for p in pieces]
    grad_query = jnp.concatenate(
        in_order([pieces[0] + pieces[2], pieces[1] + pieces[3]], core), axis=1
    ).astype(bf16)
    grad_input, gain_two = rms_pull(stream_one, gain_values[1], mm(grad_query, cross_query, NT))
    grad_rows = grad_rows + grad_input

    def core_halves(parts):
        parts = parts.reshape(-1, chips, 2, shard, width)
        kept = lax.dynamic_index_in_dim(parts, core, 2, keepdims=False)
        return kept, send(lax.dynamic_index_in_dim(parts, 1 - core, 2, keepdims=False), (1, 0))

    def chip_sum(parts):
        pieces = chip_pieces(parts.transpose(1, 0, 2, 3), chip)
        return sum(p.astype(f32) for p in pieces)

    query_part = mm(after(hidden_two, grad_rows), grad_query, TN).astype(bf16)
    kept, came = core_halves(jnp.stack([query_part, exit_cross_part]))
    pair_kept, pair_came = core_halves(pair_part)
    cross_sums = (kept.astype(f32) + came.astype(f32)).astype(bf16)
    cross_chips = jnp.concatenate([cross_sums, *in_order([pair_kept, pair_came], core)], axis=0)

    grad_low = grad_rows.astype(bf16)
    grad_self = mm(grad_low, exit_self_t).astype(bf16)
    output = rows_beside(after(output, grad_self)).astype(f32)
    by_columns = jnp.stack([grad_self[:, s * local : (s + 1) * local] for s in range(4)])
    pieces = member_pieces(lambda d: pick(by_columns, columns ^ (2 * (d & 1) + (d >> 1))))
    grad_self = jnp.pad(
        jnp.concatenate(in_order(pieces, member), axis=0), ((0, 0), (0, 256 - local))
    )
    second_grads = jnp.concatenate(
        [second_grads[:, h * 3 * hidden : (h + 1) * 3 * hidden] for h in range(head_count)], axis=0
    )
    grad_self = after(grad_self, second_grads)
    second_grads = lax.psum_scatter(second_grads, "head", scatter_dimension=0, tiled=True)
    second_grads = second_grads.astype(f32)
    grad_qkv = self_backward(qkv, grad_self, self_out, self_sums, starts)
    grad_normed = mm(grad_qkv, self_weights, NT)
    inverse = lax.rsqrt(jnp.mean(stream * stream, axis=-1, keepdims=True) + norm_eps)
    gain_one = jnp.sum(grad_normed * stream * inverse, axis=0)
    by_near = grad_normed.reshape(2, 2, row_count, width)
    kept = lax.dynamic_index_in_dim(by_near, core, 1, keepdims=False)
    came = lax.dynamic_index_in_dim(by_near, 1 - core, 1, keepdims=False).astype(bf16)
    self_core = mm(after(hidden_one, came), grad_qkv, TN).astype(bf16)
    kept = after(kept, self_core) + send(came, (1, 0)).astype(f32)
    came = send(pick(kept, 1 - near).astype(bf16), (0, 1))
    cross_chips = after(cross_chips, kept)
    cross_sums = chip_sum(cross_chips)
    memory_sum = after(memory_part[:, 0], cross_chips) + memory_came.astype(f32)
    memory_sum = memory_sum.astype(bf16)
    memory_sum = across(memory_sum)
    grad_normed = pick(kept, near) + came.astype(f32)
    grad_input, _ = rms_pull(stream_rows, gain_values[0], grad_normed)
    token_grads = (grad_rows + grad_input).astype(bf16)

    exit_self_part = mm(after(grad_low, token_grads), self_rows, TN).astype(bf16)
    kept, came = core_halves(exit_self_part)
    gain_part = jnp.stack([gain_one, gain_two, gain_three], axis=1).astype(bf16)
    gain_part = jnp.pad(gain_part, ((0, 0), (0, width - 3 * local - 3)))
    self_part = jnp.concatenate(
        [self_core[:, 256 * s : 256 * s + local] for s in range(3)] + [after(gain_part, token_grads)],
        axis=1,
    )
    self_part = self_part.reshape(chips, 2, shard, width)
    mine = lax.dynamic_index_in_dim(self_part, core, 1, keepdims=False)
    theirs = send(lax.dynamic_index_in_dim(self_part, 1 - core, 1, keepdims=False), (1, 0))
    token_grads = rows_within(token_grads)
    cross_sums = after(cross_sums, token_grads)
    token_grads = rows_across(token_grads)
    self_sums = jnp.stack(in_order([mine, theirs], core))
    self_sums = jnp.concatenate(
        [(kept.astype(f32) + came.astype(f32)).astype(bf16), self_sums], axis=0
    )
    self_sums = after(self_sums, cross_sums)
    token_grads = after(token_grads, self_sums, second_grads)
    self_sums = chip_sum(self_sums)

    sums = jnp.concatenate([self_sums[0:1], cross_sums, self_sums[1:3]], axis=0)
    sums = after(sums, token_grads, memory_sum)
    memory_grads = memory_sum.reshape(IMG_DEV, dp_count, patch_local, width).transpose(1, 0, 2, 3)
    memory_grads = lax.all_to_all(
        memory_grads.reshape(dp_count, IMG_DEV * patch_local, width),
        "dp",
        split_axis=0,
        concat_axis=0,
        tiled=True,
    )
    memory_grads = memory_grads.reshape(memory.shape).astype(f32)
    token_grads = rows_beside(token_grads).astype(f32)

    by_head = jnp.stack(
        [
            jnp.stack(
                [sums[w, :, h * local : (h + 1) * local] for w in range(3)]
                + [
                    sums[
                        3 + h // 2,
                        :,
                        w * half_width + (h % 2) * local : w * half_width + (h % 2 + 1) * local,
                    ]
                    for w in range(2)
                ]
                + [sums[5, :, 3 * local :] + sums[6, :, 3 * local :]]
            )
            for h in range(head_count)
        ]
    )
    by_head = by_head.reshape(2, 2, 6, shard, local)
    kept = lax.dynamic_index_in_dim(by_head, near, 1, keepdims=False)
    came = lax.dynamic_index_in_dim(by_head, 1 - near, 1, keepdims=False)
    kept = kept + send(came.astype(bf16), (0, 1)).astype(f32)
    self_grads = sums[5] + send(sums[6].astype(bf16), (0, 2)).astype(f32)
    first_grads = pick(kept, side) + send(pick(kept, 1 - side).astype(bf16), (0, 2)).astype(f32)
    exit_grads = jnp.stack([first_grads[0].T, first_grads[2].T])
    expand_grads = jnp.stack([second_grads[:, 0:hidden], second_grads[:, hidden : 2 * hidden]])
    contract_grads = second_grads[:, 2 * hidden :].T

    gain_grads = first_grads[5, :, 0:3].T
    entry_grads = jnp.stack(
        [self_grads[:, s * local : (s + 1) * local] for s in range(3)]
        + [first_grads[w] for w in (1, 3, 4)]
    )

    entry_mean, entry_square, entry_step = lamb_step(
        entry_weights, entry_grads, entry_first, entry_second, weight_decay
    )
    exit_mean, exit_square, exit_step = lamb_step(
        exit_weights, exit_grads, exit_first, exit_second, weight_decay
    )
    expand_mean, expand_square, expand_step = lamb_step(
        expand_weights, expand_grads, expand_first, expand_second, weight_decay
    )
    contract_mean, contract_square, contract_step = lamb_step(
        contract_weights, contract_grads, contract_first, contract_second, weight_decay
    )
    gains_mean, gains_square, gains_step = lamb_step(
        norm_gains, gain_grads, gains_first, gains_second, 0.0
    )
    weight_local = jnp.concatenate(
        [
            jnp.sum(entry_weights * entry_weights, axis=(1, 2)),
            jnp.sum(exit_weights * exit_weights, axis=(1, 2)),
            jnp.sum(expand_weights * expand_weights, axis=(1, 2)),
            jnp.sum(contract_weights * contract_weights).reshape(1),
            jnp.sum(norm_gains * norm_gains, axis=1) / head_count,
        ]
    )
    step_local = jnp.concatenate(
        [
            jnp.sum(entry_step * entry_step, axis=(1, 2)),
            jnp.sum(exit_step * exit_step, axis=(1, 2)),
            jnp.sum(expand_step * expand_step, axis=(1, 2)),
            jnp.sum(contract_step * contract_step).reshape(1),
            jnp.sum(gains_step * gains_step, axis=1) / head_count,
        ]
    )
    weight_squares, step_squares = all_sum(after(jnp.stack([weight_local, step_local]), token_grads, memory_grads))
    weight_norm = jnp.sqrt(weight_squares)
    step_norm = jnp.sqrt(step_squares)
    ratio = learn_rate * weight_norm / (step_norm + adam_eps)
    entry_new = entry_weights - ratio[0:6][:, None, None] * entry_step
    exit_new = exit_weights - ratio[6:8][:, None, None] * exit_step
    expand_new = expand_weights - ratio[8:10][:, None, None] * expand_step
    contract_new = contract_weights - ratio[10] * contract_step
    gains_new = norm_gains - ratio[11:14][:, None] * gains_step
    trust_norms = jnp.stack([weight_norm, step_norm])
    return (
        output,
        token_grads,
        memory_grads,
        entry_grads,
        exit_grads,
        expand_grads,
        contract_grads,
        gain_grads,
        entry_mean,
        exit_mean,
        expand_mean,
        contract_mean,
        gains_mean,
        entry_square,
        exit_square,
        expand_square,
        contract_square,
        gains_square,
        entry_new,
        exit_new,
        expand_new,
        contract_new,
        gains_new,
        entry_new.astype(jnp.bfloat16),
        exit_new.astype(jnp.bfloat16),
        expand_new.astype(jnp.bfloat16),
        contract_new.astype(jnp.bfloat16),
        trust_norms,
    )


def solution(mesh):
    in_specs = (
        P("dp", None),
        P(None, ("dp", "head"), None),
        P("dp", None),
        P("dp"),
        P("dp"),
        P("dp"),
        P(None, "dp", "head"),
        P(None, "head", "dp"),
        P(None, "dp", "head"),
        P("head", "dp"),
        P(None, "dp"),
        P(None, "dp", "head"),
        P(None, "dp", "head"),
        P(None, "head", "dp"),
        P(None, "head", "dp"),
        P(None, "dp", "head"),
        P(None, "dp", "head"),
        P("head", "dp"),
        P("head", "dp"),
        P(None, "dp"),
        P(None, "dp"),
    )
    out_specs = (
        P("dp", None),
        P("dp", None),
        P(None, ("dp", "head"), None),
        P(None, "dp", "head"),
        P(None, "head", "dp"),
        P(None, "dp", "head"),
        P("head", "dp"),
        P(None, "dp"),
        P(None, "dp", "head"),
        P(None, "head", "dp"),
        P(None, "dp", "head"),
        P("head", "dp"),
        P(None, "dp"),
        P(None, "dp", "head"),
        P(None, "head", "dp"),
        P(None, "dp", "head"),
        P("head", "dp"),
        P(None, "dp"),
        P(None, "dp", "head"),
        P(None, "head", "dp"),
        P(None, "dp", "head"),
        P("head", "dp"),
        P(None, "dp"),
        P(None, "dp", "head"),
        P(None, "head", "dp"),
        P(None, "dp", "head"),
        P("head", "dp"),
        P(),
    )
    return jax.shard_map(
        per_device, mesh=mesh, in_specs=in_specs, out_specs=out_specs, check_vma=False
    )
```

```python
import jax
import jax.numpy as jnp
from jax import lax
from jax.experimental import pallas as pl
from jax.experimental.pallas import tpu as pltpu
from jax.sharding import PartitionSpec as P

HEAD_DIM = 64
IMG_DEV = 2
STEPS_DONE = 10


group_scale = (1.0, 0.5, 2.0)
first_decay = 0.9
second_decay = 0.999
learn_rate = 0.5
weight_decay = 0.01
adam_eps = 1e-06
norm_eps = 1e-06
masked_score = -1e30


def token_layout(lengths, groups, image_map, tok_rows, img_count):
    text_count = lengths.shape[1]
    text_ends = jnp.cumsum(lengths, axis=1)
    position = jnp.arange(tok_rows, dtype=jnp.int32)
    segment = jnp.sum((position[None, :, None] >= text_ends[:, None, :]).astype(jnp.int32), axis=2)
    chosen = (segment[:, :, None] == jnp.arange(text_count, dtype=jnp.int32)[None, None, :]).astype(
        jnp.int32
    )
    group_tok = jnp.sum(chosen * groups[:, None, :], axis=2)
    image_tok = jnp.sum(chosen * (image_map % img_count)[:, None, :], axis=2)
    scale_table = jnp.array(group_scale, dtype=jnp.float32)
    picked = (group_tok[:, :, None] == jnp.arange(3, dtype=jnp.int32)[None, None, :]).astype(
        jnp.float32
    )
    weight_tok = jnp.sum(picked * scale_table, axis=2) * (segment < text_count).astype(jnp.float32)
    return (segment, image_tok, weight_tok)


def rms_norm(values, gain):
    return values * lax.rsqrt(jnp.mean(values * values, axis=-1, keepdims=True) + norm_eps) * gain


def gated_hidden(gate, upward):
    return jax.nn.gelu(gate, approximate=True) * upward


BLOCK = 256
LANES = 128
LOG2E = 1.4426950408889634
NT = (((1,), (1,)), ((), ()))
TN = (((0,), (0,)), ((), ()))
VMEM_LIMIT = 50 * 1024 * 1024


def mm(a, b, dims=(((1,), (0,)), ((), ()))):
    return lax.dot_general(a, b, dims, preferred_element_type=jnp.float32)


def half_lanes(block, half):
    lane = lax.broadcasted_iota(jnp.int32, (1, LANES), 1)
    return jnp.where((lane // HEAD_DIM) == half, block, jnp.zeros_like(block))


def span_mask(start_ref, block, keys):
    low = block * BLOCK
    key_pos = lax.broadcasted_iota(jnp.int32, (keys, BLOCK), 0)
    query_pos = low + lax.broadcasted_iota(jnp.int32, (keys, BLOCK), 1)
    return (key_pos >= start_ref[0:1, low : low + BLOCK]) & (key_pos <= query_pos)


def self_forward_kernel(qkv_ref, start_ref, out_ref, sums_ref):
    rows = qkv_ref.shape[0]
    scale = HEAD_DIM ** (-0.5)
    sums_ref[...] = jnp.zeros_like(sums_ref)
    for pair in range(2):
        lanes = slice(LANES * pair, LANES * (pair + 1))
        for block in range(rows // BLOCK):
            own = slice(block * BLOCK, (block + 1) * BLOCK)
            keys = (block + 1) * BLOCK
            key_set = qkv_ref[0:keys, 256 + LANES * pair : 256 + LANES * (pair + 1)]
            value_set = qkv_ref[0:keys, 512 + LANES * pair : 512 + LANES * (pair + 1)]
            query_set = qkv_ref[own, lanes]
            allowed = span_mask(start_ref, block, keys)
            pieces = []
            for half in range(2 - pair):
                scores = mm(key_set, half_lanes(query_set, half), NT)
                scores = jnp.where(allowed, scores, masked_score)
                largest = jnp.max(scores, axis=0, keepdims=True)
                weights = jnp.exp2((scores - largest) * (scale * LOG2E))
                total = jnp.sum(weights, axis=0, keepdims=True)
                mixed = mm(value_set, weights.astype(jnp.bfloat16), TN) / total
                pieces.append(mixed[half * HEAD_DIM : (half + 1) * HEAD_DIM])
                row = 2 * pair + half
                sums_ref[row : row + 1, own] = largest * scale + jnp.log(total)
            if pair == 1:
                pieces.append(jnp.zeros_like(pieces[0]))
            out_ref[own, lanes] = jnp.concatenate(pieces, axis=0).T.astype(jnp.bfloat16)


def self_forward(qkv, starts):
    rows = qkv.shape[0]
    return pl.pallas_call(
        self_forward_kernel,
        out_shape=(
            jax.ShapeDtypeStruct((rows, 256), jnp.bfloat16),
            jax.ShapeDtypeStruct((8, rows), jnp.float32),
        ),
        compiler_params=pltpu.CompilerParams(vmem_limit_bytes=VMEM_LIMIT),
        cost_estimate=pl.CostEstimate(
            flops=6 * 10**9, bytes_accessed=rows * 2048, transcendentals=2 * rows * rows
        ),
        name="self_forward",
    )(qkv, starts)


def self_backward_kernel(
    qkv_ref, grad_ref, out_ref, sums_ref, start_ref, result_ref, key_acc, value_acc
):
    rows = qkv_ref.shape[0]
    scale = HEAD_DIM ** (-0.5)
    for pair in range(2):
        lanes = slice(LANES * pair, LANES * (pair + 1))
        key_lanes = slice(256 + LANES * pair, 256 + LANES * (pair + 1))
        value_lanes = slice(512 + LANES * pair, 512 + LANES * (pair + 1))
        for block in reversed(range(rows // BLOCK)):
            own = slice(block * BLOCK, (block + 1) * BLOCK)
            keys = (block + 1) * BLOCK
            key_set = qkv_ref[0:keys, key_lanes]
            value_set = qkv_ref[0:keys, value_lanes]
            query_set = qkv_ref[own, lanes]
            grad_set = grad_ref[own, lanes]
            allowed = span_mask(start_ref, block, keys)
            product = (
                grad_set.astype(jnp.float32) * out_ref[own, lanes].astype(jnp.float32)
            ).T
            pieces = []
            key_part = None
            for half in range(2 - pair):
                row = 2 * pair + half
                inner = jnp.sum(
                    product[half * HEAD_DIM : (half + 1) * HEAD_DIM], axis=0, keepdims=True
                )
                query_half = half_lanes(query_set, half)
                grad_half = half_lanes(grad_set, half)
                scores = mm(key_set, query_half, NT)
                probs = jnp.where(
                    allowed,
                    jnp.exp2(scores * (scale * LOG2E) - sums_ref[row : row + 1, own] * LOG2E),
                    0.0,
                )
                grad_probs = mm(value_set, grad_half, NT)
                grad_scores = (probs * (grad_probs - inner)).astype(jnp.bfloat16)
                value_new = mm(probs.astype(jnp.bfloat16), grad_half)
                key_new = mm(grad_scores, query_half)
                key_part = key_new if key_part is None else key_part + key_new
                value_part = value_new if half == 0 else value_part + value_new
                mixed = mm(key_set, grad_scores, TN) * scale
                pieces.append(mixed[half * HEAD_DIM : (half + 1) * HEAD_DIM])
            if pair == 1:
                pieces.append(jnp.zeros_like(pieces[0]))
            result_ref[own, lanes] = jnp.concatenate(pieces, axis=0).T.astype(jnp.bfloat16)
            if keys == rows:
                key_acc[...] = key_part
                value_acc[...] = value_part
            else:
                key_acc[0:keys, :] += key_part
                value_acc[0:keys, :] += value_part
        result_ref[:, key_lanes] = (key_acc[...] * scale).astype(jnp.bfloat16)
        result_ref[:, value_lanes] = value_acc[...].astype(jnp.bfloat16)


def self_backward(qkv, grad_out, out, sums, starts):
    rows = qkv.shape[0]
    return pl.pallas_call(
        self_backward_kernel,
        out_shape=jax.ShapeDtypeStruct((rows, 768), jnp.bfloat16),
        scratch_shapes=[
            pltpu.VMEM((rows, LANES), jnp.float32),
            pltpu.VMEM((rows, LANES), jnp.float32),
        ],
        compiler_params=pltpu.CompilerParams(vmem_limit_bytes=VMEM_LIMIT),
        cost_estimate=pl.CostEstimate(
            flops=8 * 10**9, bytes_accessed=rows * 5120, transcendentals=2 * rows * rows
        ),
        name="self_backward",
    )(qkv, grad_out, out, sums, starts)


def image_blocks(split, image, blocks):
    if image == 0:
        return 0, (split + BLOCK - 1) // BLOCK
    return split // BLOCK, blocks


def own_columns(split, image, low):
    column = low + lax.broadcasted_iota(jnp.int32, (1, BLOCK), 1)
    return column < split if image == 0 else column >= split


def own_rows(split, image, low):
    row = low + lax.broadcasted_iota(jnp.int32, (BLOCK, LANES), 0)
    return row < split if image == 0 else row >= split


def cross_forward_kernel(split_ref, query_ref, key_ref, value_ref, out_ref, sums_ref):
    rows = query_ref.shape[0]
    keys = key_ref.shape[0] // IMG_DEV
    scale = HEAD_DIM ** (-0.5)
    split = split_ref[0]
    for image in range(IMG_DEV):
        first, last = image_blocks(split, image, rows // BLOCK)

        def step(block, carry):
            low = pl.multiple_of(block * BLOCK, BLOCK)
            query_set = query_ref[pl.ds(low, BLOCK), :]
            key_set = key_ref[image * keys : (image + 1) * keys, :]
            value_set = value_ref[image * keys : (image + 1) * keys, :]
            kept = own_columns(split, image, low)
            halves = jnp.concatenate([half_lanes(query_set, half) for half in range(2)], axis=0)
            scores = mm(key_set, halves, NT)
            largest = jnp.max(scores, axis=0, keepdims=True)
            weights = jnp.exp2((scores - largest) * (scale * LOG2E))
            total = jnp.sum(weights, axis=0, keepdims=True)
            mixed = mm(value_set, weights.astype(jnp.bfloat16), TN) / total
            logs = largest * scale + jnp.log(total)
            pieces = []
            for half in range(2):
                own = slice(half * BLOCK, (half + 1) * BLOCK)
                pieces.append(mixed[half * HEAD_DIM : (half + 1) * HEAD_DIM, own])
                held = sums_ref[0, half : half + 1, pl.ds(low, BLOCK)]
                sums_ref[0, half : half + 1, pl.ds(low, BLOCK)] = jnp.where(
                    kept, logs[:, own], held
                )
            fresh = jnp.concatenate(pieces, axis=0).T
            held = out_ref[pl.ds(low, BLOCK), :].astype(jnp.float32)
            out_ref[pl.ds(low, BLOCK), :] = jnp.where(
                own_rows(split, image, low), fresh, held
            ).astype(jnp.bfloat16)
            return carry

        lax.fori_loop(first, last, step, 0)


def cross_forward(split, queries, pairs):
    rows, width = queries.shape
    keys = pairs.shape[0]
    groups = width // LANES
    return pl.pallas_call(
        cross_forward_kernel,
        grid=(groups,),
        in_specs=[
            pl.BlockSpec(memory_space=pltpu.SMEM),
            pl.BlockSpec((rows, LANES), lambda j: (0, j)),
            pl.BlockSpec((keys, LANES), lambda j: (0, j)),
            pl.BlockSpec((keys, LANES), lambda j: (0, groups + j)),
        ],
        out_specs=(
            pl.BlockSpec((rows, LANES), lambda j: (0, j)),
            pl.BlockSpec((1, 8, rows), lambda j: (j, 0, 0)),
        ),
        out_shape=(
            jax.ShapeDtypeStruct((rows, width), jnp.bfloat16),
            jax.ShapeDtypeStruct((groups, 8, rows), jnp.float32),
        ),
        compiler_params=pltpu.CompilerParams(vmem_limit_bytes=VMEM_LIMIT),
        cost_estimate=pl.CostEstimate(
            flops=28 * 10**9,
            bytes_accessed=keys * 1536,
            transcendentals=groups * rows * keys,
        ),
        name="cross_forward",
    )(split, queries, pairs, pairs)


def cross_backward_kernel(
    split_ref,
    query_ref,
    grad_ref,
    stats_ref,
    key_ref,
    value_ref,
    query_out,
    key_out,
    value_out,
    key_acc,
    value_acc,
):
    rows = query_ref.shape[0]
    keys = key_ref.shape[0] // IMG_DEV
    scale = HEAD_DIM ** (-0.5)
    split = split_ref[0]
    for image in range(IMG_DEV):
        first, last = image_blocks(split, image, rows // BLOCK)
        span = slice(image * keys, (image + 1) * keys)
        key_acc[...] = jnp.zeros_like(key_acc)
        value_acc[...] = jnp.zeros_like(value_acc)

        def step(block, carry):
            low = pl.multiple_of(block * BLOCK, BLOCK)
            query_set = query_ref[pl.ds(low, BLOCK), :]
            grad_set = grad_ref[pl.ds(low, BLOCK), :]
            key_set = key_ref[span, :]
            value_set = value_ref[span, :]
            kept = own_columns(split, image, low)
            shifts, inners = [], []
            for half in range(2):
                sums = stats_ref[0, half : half + 1, pl.ds(low, BLOCK)]
                inners.append(stats_ref[0, 2 + half : 3 + half, pl.ds(low, BLOCK)])
                shifts.append(jnp.where(kept, sums * LOG2E, -masked_score))
            shift = jnp.concatenate(shifts, axis=1)
            inner = jnp.concatenate(inners, axis=1)
            queries = jnp.concatenate([half_lanes(query_set, half) for half in range(2)], axis=0)
            grads = jnp.concatenate([half_lanes(grad_set, half) for half in range(2)], axis=0)
            scores = mm(key_set, queries, NT)
            probs = jnp.exp2(scores * (scale * LOG2E) - shift)
            grad_probs = mm(value_set, grads, NT)
            grad_scores = (probs * (grad_probs - inner)).astype(jnp.bfloat16)
            value_acc[...] += mm(probs.astype(jnp.bfloat16), grads)
            key_acc[...] += mm(grad_scores, queries)
            mixed = mm(key_set, grad_scores, TN) * scale
            pieces = [
                mixed[half * HEAD_DIM : (half + 1) * HEAD_DIM, half * BLOCK : (half + 1) * BLOCK]
                for half in range(2)
            ]
            fresh = jnp.concatenate(pieces, axis=0).T
            held = query_out[pl.ds(low, BLOCK), :].astype(jnp.float32)
            query_out[pl.ds(low, BLOCK), :] = jnp.where(
                own_rows(split, image, low), fresh, held
            ).astype(jnp.bfloat16)
            return carry

        lax.fori_loop(first, last, step, 0)
        key_out[span, :] = (key_acc[...] * scale).astype(jnp.bfloat16)
        value_out[span, :] = value_acc[...].astype(jnp.bfloat16)


def cross_backward(split, queries, grads, stats, pairs):
    rows, width = queries.shape
    keys = pairs.shape[0]
    groups = width // LANES
    return pl.pallas_call(
        cross_backward_kernel,
        grid=(groups,),
        in_specs=[
            pl.BlockSpec(memory_space=pltpu.SMEM),
            pl.BlockSpec((rows, LANES), lambda j: (0, j)),
            pl.BlockSpec((rows, LANES), lambda j: (0, j)),
            pl.BlockSpec((1, 8, rows), lambda j: (j, 0, 0)),
            pl.BlockSpec((keys, LANES), lambda j: (0, j)),
            pl.BlockSpec((keys, LANES), lambda j: (0, groups + j)),
        ],
        out_specs=(
            pl.BlockSpec((rows, LANES), lambda j: (0, j)),
            pl.BlockSpec((keys, LANES), lambda j: (0, j)),
            pl.BlockSpec((keys, LANES), lambda j: (0, j)),
        ),
        out_shape=(
            jax.ShapeDtypeStruct((rows, width), jnp.bfloat16),
            jax.ShapeDtypeStruct((keys, width), jnp.bfloat16),
            jax.ShapeDtypeStruct((keys, width), jnp.bfloat16),
        ),
        scratch_shapes=[
            pltpu.VMEM((keys // IMG_DEV, LANES), jnp.float32),
            pltpu.VMEM((keys // IMG_DEV, LANES), jnp.float32),
        ],
        compiler_params=pltpu.CompilerParams(vmem_limit_bytes=VMEM_LIMIT),
        cost_estimate=pl.CostEstimate(
            flops=28 * 10**9,
            bytes_accessed=keys * 3072,
            transcendentals=groups * rows * keys,
        ),
        name="cross_backward",
    )(split, queries, grads, stats, pairs, pairs)


def hidden_grads_kernel(rows_ref, grad_ref, gate_ref, up_ref, act_ref, out_ref):
    part = pl.program_id(0)
    source = (gate_ref, up_ref, act_ref)
    for index in range(3):

        @pl.when(part == index)
        def _():
            left = grad_ref if index == 2 else rows_ref
            out_ref[...] = mm(left[...], source[index][...], TN).astype(jnp.bfloat16)


def hidden_grads(rows, grads, gate, upward, act):
    row_count, width = rows.shape
    inner_width = gate.shape[1]
    blocks = lax.axis_size("head")
    block = inner_width // blocks
    whole = pl.BlockSpec((row_count, width), lambda p, j: (0, 0))

    def column(index):
        return pl.BlockSpec(
            (row_count, block), lambda p, j: (0, jnp.clip((p - index) * blocks + j, 0, blocks - 1))
        )

    return pl.pallas_call(
        hidden_grads_kernel,
        grid=(3, blocks),
        in_specs=[whole, whole, column(0), column(1), column(2)],
        out_specs=pl.BlockSpec((width, block), lambda p, j: (0, j * 3 + p)),
        out_shape=jax.ShapeDtypeStruct((width, 3 * inner_width), jnp.bfloat16),
        compiler_params=pltpu.CompilerParams(vmem_limit_bytes=VMEM_LIMIT),
        cost_estimate=pl.CostEstimate(
            flops=6 * row_count * width * inner_width,
            bytes_accessed=6 * width * inner_width,
            transcendentals=0,
        ),
        name="hidden_grads",
    )(rows, grads, gate, upward, act)


def rms_pull(values, gain, grad):
    inverse = lax.rsqrt(jnp.mean(values * values, axis=-1, keepdims=True) + norm_eps)
    hat = values * inverse
    scaled = grad * gain
    inner = jnp.mean(scaled * hat, axis=-1, keepdims=True)
    return inverse * (scaled - hat * inner), jnp.sum(grad * hat, axis=0)


def two_terms(values):
    high = lax.reduce_precision(values, exponent_bits=8, mantissa_bits=7)
    return high.astype(jnp.bfloat16), (values - high).astype(jnp.bfloat16)


def after(array, *earlier):
    marks = [e[(0,) * e.ndim].astype(jnp.float32) for e in earlier]
    mark = sum(marks[1:], marks[0])
    return jnp.where(mark == mark, array, jnp.asarray(jnp.nan, array.dtype))


def pick(array, index):
    return lax.dynamic_index_in_dim(array, index, 0, keepdims=False)


def send(array, bits, axis=("dp", "head")):
    dp_count = lax.axis_size("dp")
    head_count = lax.axis_size("head")
    dp_bits, head_bits = bits
    if head_bits == 0:
        return lax.ppermute(array, "dp", [(s, s ^ dp_bits) for s in range(dp_count)])
    if dp_bits == 0:
        return lax.ppermute(array, "head", [(s, s ^ head_bits) for s in range(head_count)])
    pairs = [
        (i * head_count + h, (i ^ dp_bits) * head_count + (h ^ head_bits))
        for i in range(dp_count)
        for h in range(head_count)
    ]
    return lax.ppermute(array, ("dp", "head"), pairs)


def in_order(pieces, index):
    bit = 1
    while bit < len(pieces):
        flip = (index & bit) != 0
        pieces = [jnp.where(flip, pieces[s ^ bit], pieces[s]) for s in range(len(pieces))]
        bit *= 2
    return pieces


def head_spread(block, far, late=None):
    head_count = lax.axis_size("head")
    head_index = lax.axis_index("head")
    held = jnp.stack(in_order([block, far], head_index // 2))
    came = send(held, (0, 1))
    came = came if late is None else after(came, late)
    lower, upper = in_order([held, came], head_index % 2)
    return [(lower, upper)[h % 2][h // 2] for h in range(head_count)]


def chip_pieces(blocks, chip):
    return [pick(blocks, chip)] + [
        send(pick(blocks, chip ^ d), (2 * d, 0)) for d in range(1, blocks.shape[0])
    ]


def chip_spread(block, chip):
    chips = lax.axis_size("dp") // 2
    return in_order([block] + [send(block, (2 * d, 0)) for d in range(1, chips)], chip)


def member_pieces(block_of):
    return [block_of(0)] + [send(block_of(d), (d & 1, d >> 1)) for d in range(1, 4)]


def head_halving(blocks):
    head_count = lax.axis_size("head")
    index = lax.axis_index("head")
    low, high = index % 2, index // 2
    by_low = blocks.reshape(head_count // 2, 2, *blocks.shape[1:])
    mine = lax.dynamic_index_in_dim(by_low, low, 1, keepdims=False)
    theirs = lax.dynamic_index_in_dim(by_low, 1 - low, 1, keepdims=False)
    both = mine.astype(jnp.float32) + send(theirs, (0, 1)).astype(jnp.float32)
    sent = both.astype(blocks.dtype)
    total = pick(both, high)
    for d in range(1, head_count // 2):
        total = total + send(pick(sent, high ^ d), (0, 2 * d)).astype(jnp.float32)
    return total


def all_sum(values):
    total = values + send(values, (1, 0))
    total = sum(chip_spread(total, lax.axis_index("dp") // 2))
    return sum(head_spread(total, send(total, (0, 2))))
def lamb_step(weight, grad, first, second, decay):
    mean = first_decay * first + (1.0 - first_decay) * grad
    square = second_decay * second + (1.0 - second_decay) * grad * grad
    step = (
        mean
        / (1.0 - first_decay**STEPS_DONE)
        / (jnp.sqrt(square / (1.0 - second_decay**STEPS_DONE)) + adam_eps)
        + decay * weight
    )
    return (mean, square, step)


def per_device(
    tokens,
    memory,
    cotangent,
    lengths,
    groups,
    image_map,
    entry_weights,
    exit_weights,
    expand_weights,
    contract_weights,
    norm_gains,
    entry_first,
    entry_second,
    exit_first,
    exit_second,
    expand_first,
    expand_second,
    contract_first,
    contract_second,
    gains_first,
    gains_second,
):
    dp_count = lax.axis_size("dp")
    head_count = lax.axis_size("head")
    dp_index = lax.axis_index("dp")
    head_index = lax.axis_index("head")
    chips = dp_count // 2
    chip, core = dp_index // 2, dp_index % 2
    side, near = head_index // 2, head_index % 2
    member = 2 * near + core
    here = core == side
    bf16 = jnp.bfloat16
    f32 = jnp.float32
    tok_rows, width = tokens.shape
    half_width = width // 2
    local = entry_weights.shape[2]
    hidden = expand_weights.shape[2]
    shard = width // dp_count
    row_count = tok_rows // 4
    image_count, patch_local = memory.shape[0:2]
    heads = local // HEAD_DIM

    def quarter(array):
        return pick(array.reshape(4, row_count, *array.shape[1:]), member)

    layout = jnp.stack([lengths, groups, image_map])
    layout = jnp.where(here, layout, send(layout, (1, 0)))
    stream_low = jnp.where(here, tokens, send(tokens, (1, 0)))
    other_rows = pick(cotangent.reshape(4, row_count, width), member ^ 1)
    cotangent_rows = jnp.where(here, quarter(cotangent), send(other_rows, (1, 0)))

    segments, images, weights = token_layout(
        layout[0:1], layout[1:2], layout[2:3], tok_rows, IMG_DEV
    )
    image_tok = images[0]
    weight_tok = weights[0]
    text_ends = jnp.cumsum(layout[0])
    position = jnp.arange(tok_rows, dtype=jnp.int32)
    starts = jnp.max(
        jnp.where(position[None, :] >= text_ends[:, None], text_ends[:, None], 0), axis=0
    ).reshape(1, tok_rows)
    of_zero = (image_tok == 0).astype(jnp.int32)
    before = jnp.cumsum(of_zero)
    split = before[-1]
    place = jnp.where(image_tok == 0, before - 1, split + position - before)
    sorter = (place[None, :] == position[:, None]).astype(bf16)
    unsorter = (place[:, None] == position[None, :]).astype(bf16)
    split = split.reshape(1)

    entry_low = entry_weights.astype(bf16).transpose(1, 0, 2)
    exit_low = exit_weights.astype(bf16).transpose(2, 0, 1)
    expand_low = expand_weights.astype(bf16).transpose(1, 0, 2)
    contract_low = contract_weights.astype(bf16).transpose(1, 0)[:, None]
    gains_low = jnp.pad(norm_gains.astype(bf16).transpose(1, 0), ((0, 0), (0, HEAD_DIM - 3)))

    def across(array):
        pairs = [
            (i * head_count + h, (i ^ 1) * head_count + (h ^ 2))
            for i in range(dp_count)
            for h in range(head_count)
            if i % 2 != h // 2
        ]
        return jnp.where(here, array, lax.ppermute(array, ("dp", "head"), pairs))

    moved = lax.all_to_all(
        memory.reshape(dp_count, IMG_DEV * patch_local, width),
        "dp",
        split_axis=0,
        concat_axis=0,
        tiled=True,
    )
    patches = dp_count * patch_local
    moved = moved.reshape(dp_count, IMG_DEV, patch_local, width).transpose(1, 0, 2, 3)
    moved = moved.reshape(IMG_DEV, patches, width)
    held = across(moved)
    other = send(held, (1, 0))
    memory_pair = jnp.concatenate([held, other], axis=1)
    memory_pair = memory_pair.reshape(2 * IMG_DEV * patches, width)

    own_set = entry_low[:, 0:3].reshape(shard, 3 * local)
    rest_set = jnp.concatenate([exit_low[:, 0:1], entry_low[:, 3:6], exit_low[:, 1:2]], axis=1)
    rest_set = rest_set.reshape(shard, 5 * local)
    far_set = send(jnp.concatenate([own_set, rest_set], axis=1), (0, 2))
    far_set = after(far_set, moved)
    far_set, far_rest = far_set[:, 0 : 3 * local], far_set[:, 3 * local :]
    mine = jnp.where(core == 0, own_set, far_set)
    theirs = jnp.where(core == 0, far_set, own_set)
    mine = jnp.concatenate([mine, gains_low], axis=1)
    theirs = send(jnp.concatenate([theirs, gains_low], axis=1), (1, 0))

    rest_set = jnp.stack(head_spread(rest_set, far_rest)).reshape(head_count, shard, 5, local)
    rest_set = rest_set.transpose(1, 2, 0, 3).reshape(shard, 5 * width)
    rest_full = lax.all_gather(rest_set, "dp", axis=0, tiled=True)
    exit_self_t = rest_full[:, 0:width]
    cross_query = rest_full[:, width : 2 * width]
    cross_pair = jnp.concatenate(
        [
            jnp.where(
                core == 0,
                rest_full[:, w * width : w * width + half_width],
                rest_full[:, w * width + half_width : (w + 1) * width],
            )
            for w in (2, 3)
        ],
        axis=1,
    )
    exit_cross_t = rest_full[:, 4 * width :]

    self_set = jnp.concatenate(in_order([mine, theirs], core), axis=0)
    self_set = after(self_set, place, weight_tok, starts)
    self_full = [after(p, held) for p in chip_spread(self_set, chip)]
    self_full = jnp.concatenate(self_full, axis=0)
    gain_values = self_full[:, 3 * local : 3 * local + 3].astype(f32).transpose(1, 0)
    self_weights = jnp.concatenate(
        [
            jnp.pad(self_full[:, s * local : (s + 1) * local], ((0, 0), (0, 256 - local)))
            for s in range(3)
        ],
        axis=1,
    )

    stream = stream_low.astype(f32)
    hidden_one = rms_norm(stream, gain_values[0]).astype(bf16)
    qkv = mm(hidden_one, self_weights).astype(bf16)
    second_set = jnp.concatenate([expand_low, contract_low], axis=1)
    far_second = send(after(second_set, held), (0, 2))
    self_out, self_sums = self_forward(qkv, starts)
    columns = jnp.where(core == 0, head_index, head_index ^ 2)

    def by_member(array, d):
        return pick(array.reshape(4, row_count, *array.shape[1:]), member ^ d)

    self_block = self_out[:, 0:local]
    pieces = member_pieces(lambda d: by_member(self_block, d))
    far_second = after(far_second, self_block)
    pieces = in_order([pieces[0], pieces[2], pieces[1], pieces[3]], columns)
    self_rows = jnp.concatenate(pieces, axis=1)
    stream_rows = quarter(stream)
    stream_one = stream_rows + mm(self_rows, exit_self_t, NT)
    hidden_two = rms_norm(stream_one, gain_values[1]).astype(bf16)
    second_set = head_spread(second_set, far_second, stream_one)
    second_set = jnp.stack(second_set, axis=2).reshape(shard, 3 * head_count * hidden)
    second_full = lax.all_gather(second_set, "dp", axis=0, tiled=True)
    inner_width = head_count * hidden
    gate_weights = second_full[:, 0:inner_width]
    up_weights = second_full[:, inner_width : 2 * inner_width]
    contract_t = second_full[:, 2 * inner_width :]

    def by_core(array, d):
        flip = core == 1 - (d & 1)
        return jnp.where(flip, array[:, half_width:], array[:, 0:half_width])

    query_rows = mm(hidden_two, cross_query).astype(bf16)
    pieces = member_pieces(lambda d: by_core(query_rows, d))
    queries = mm(sorter, jnp.concatenate(in_order(pieces, member), axis=0)).astype(bf16)
    pairs = mm(memory_pair, cross_pair).astype(bf16)
    cross_out, cross_sums = cross_forward(split, queries, pairs)
    cross_out = mm(unsorter, cross_out).astype(bf16)
    high, low = two_terms(cross_sums[:, 0:2].reshape(2 * heads, tok_rows))
    tail = jnp.concatenate([high, low, jnp.zeros((4, tok_rows), bf16)], axis=0)
    tail = mm(tail, sorter).astype(bf16)
    tail = tail.reshape(16, 4, row_count).transpose(1, 0, 2)
    tail = jnp.pad(tail, ((0, 0), (0, 0), (0, half_width - row_count)))
    blocks = jnp.concatenate([cross_out.reshape(4, row_count, half_width), tail], axis=1)
    pieces = member_pieces(lambda d: pick(blocks, member ^ d))
    spread = (
        jnp.arange(2 * heads)[:, None] == (jnp.arange(half_width) // HEAD_DIM)[None, :]
    ).astype(f32)

    def lanes_of(per_head):
        return lax.dot_general(
            per_head, spread, TN, precision=lax.Precision.HIGHEST, preferred_element_type=f32
        )

    merged = []
    merged_sums = []
    for part in ([pieces[0], pieces[2]], [pieces[1], pieces[3]]):
        sums = [
            p[row_count : row_count + 2 * heads, 0:row_count].astype(f32)
            + p[row_count + 2 * heads : row_count + 4 * heads, 0:row_count].astype(f32)
            for p in part
        ]
        largest = jnp.maximum(sums[0], sums[1])
        both = [jnp.exp(s - largest) for s in sums]
        total = both[0] + both[1]
        merged.append(
            lanes_of(both[0] / total) * part[0][0:row_count].astype(f32)
            + lanes_of(both[1] / total) * part[1][0:row_count].astype(f32)
        )
        merged_sums.append(largest + jnp.log(total))
    cross_rows = jnp.concatenate(in_order(merged, core), axis=1).astype(bf16)
    stream_two = stream_one + mm(cross_rows, exit_cross_t, NT)
    hidden_three = rms_norm(stream_two, gain_values[2]).astype(bf16)

    gate = mm(hidden_three, gate_weights)
    upward = mm(hidden_three, up_weights)
    activated, pull_gate = jax.vjp(gated_hidden, gate, upward)
    activated_low = activated.astype(bf16)
    output_rows = stream_two + mm(activated_low, contract_t, NT)
    grad_rows = cotangent_rows.astype(f32) * quarter(weight_tok)[:, None]
    grad_low = grad_rows.astype(bf16)
    grad_gate, grad_up = pull_gate(mm(grad_low, contract_t))
    grad_gate = grad_gate.astype(bf16)
    grad_up = grad_up.astype(bf16)
    act_low = grad_low
    grad_normed = mm(grad_gate, gate_weights, NT) + mm(grad_up, up_weights, NT)
    grad_input, gain_three = rms_pull(stream_two, gain_values[2], grad_normed)
    grad_rows = grad_rows + grad_input
    def rows_within(rows):
        came = send(rows, (1, 0))
        return jnp.concatenate(in_order([rows, came], core), axis=0)

    def rows_across(rows):
        pairs = [
            (i * head_count + h, i * head_count + (h ^ 2))
            for i in range(dp_count)
            for h in range(head_count)
            if i % 2 == h // 2
        ]
        return jnp.where(here, rows, lax.ppermute(rows, ("dp", "head"), pairs))

    def rows_beside(rows):
        return jnp.concatenate(in_order([rows, send(rows, (0, 1))], near), axis=0)

    output = rows_across(rows_within(output_rows.astype(bf16)))

    grad_low = grad_rows.astype(bf16)
    exit_cross_part = mm(grad_low, cross_rows, TN).astype(bf16)
    grad_cross = mm(grad_low, exit_cross_t).astype(bf16)
    product = grad_cross.astype(f32) * cross_rows.astype(f32)
    tails = []
    for g in range(2):
        inner = lax.dot_general(
            spread,
            by_core(product, g),
            NT,
            precision=lax.Precision.HIGHEST,
            preferred_element_type=f32,
        )
        tail = jnp.concatenate([*two_terms(merged_sums[g]), *two_terms(inner)], axis=0)
        tails.append(jnp.pad(tail, ((0, 32 - 8 * heads), (0, half_width - row_count))))
    pieces = member_pieces(
        lambda d: jnp.concatenate([by_core(grad_cross, d), tails[d & 1]], axis=0)
    )
    second_part = hidden_grads(after(hidden_three, pieces[1]), after(act_low, pieces[1]), grad_gate, grad_up, activated_low)
    second_grads = lax.psum_scatter(second_part, "dp", scatter_dimension=0, tiled=True)
    got = after(jnp.stack(in_order(pieces, member)), second_part)
    grads = mm(sorter, got[:, 0:row_count].reshape(tok_rows, half_width)).astype(bf16)
    stats = (
        got[:, row_count : row_count + 8 * heads, 0:row_count]
        .transpose(1, 0, 2)
        .reshape(8 * heads, tok_rows)
    )
    stats = mm(stats, unsorter)
    sums = (stats[0 : 2 * heads] + stats[2 * heads : 4 * heads]).reshape(heads, 2, tok_rows)
    inner = (stats[4 * heads : 6 * heads] + stats[6 * heads :]).reshape(heads, 2, tok_rows)
    stats = jnp.concatenate([sums, inner, jnp.zeros((heads, 4, tok_rows), f32)], axis=1)
    grad_query, grad_key, grad_value = cross_backward(split, queries, grads, stats, pairs)
    grad_query = after(mm(unsorter, grad_query).astype(bf16), output)
    grad_pair = after(jnp.concatenate([grad_key, grad_value], axis=1), grad_query)
    memory_part = mm(grad_pair, cross_pair, NT).reshape(IMG_DEV, 2, patches, width)
    memory_came = send(memory_part[:, 1].astype(bf16), (1, 0))
    pair_part = mm(memory_pair, grad_pair, TN).astype(bf16)
    pieces = member_pieces(lambda d: by_member(grad_query, d))
    pieces = [p.astype(f32) for p in pieces]
    grad_query = jnp.concatenate(
        in_order([pieces[0] + pieces[2], pieces[1] + pieces[3]], core), axis=1
    ).astype(bf16)
    grad_input, gain_two = rms_pull(stream_one, gain_values[1], mm(grad_query, cross_query, NT))
    grad_rows = grad_rows + grad_input

    def core_halves(parts):
        parts = parts.reshape(-1, chips, 2, shard, width)
        kept = lax.dynamic_index_in_dim(parts, core, 2, keepdims=False)
        return kept, send(lax.dynamic_index_in_dim(parts, 1 - core, 2, keepdims=False), (1, 0))

    def chip_sum(parts):
        pieces = chip_pieces(parts.transpose(1, 0, 2, 3), chip)
        return sum(p.astype(f32) for p in pieces)

    query_part = mm(after(hidden_two, grad_rows), grad_query, TN).astype(bf16)
    kept, came = core_halves(jnp.stack([query_part, exit_cross_part]))
    pair_kept, pair_came = core_halves(pair_part)
    cross_sums = (kept.astype(f32) + came.astype(f32)).astype(bf16)
    cross_chips = jnp.concatenate([cross_sums, *in_order([pair_kept, pair_came], core)], axis=0)

    grad_low = grad_rows.astype(bf16)
    grad_self = mm(grad_low, exit_self_t).astype(bf16)
    output = rows_beside(after(output, grad_self)).astype(f32)
    by_columns = jnp.stack([grad_self[:, s * local : (s + 1) * local] for s in range(4)])
    pieces = member_pieces(lambda d: pick(by_columns, columns ^ (2 * (d & 1) + (d >> 1))))
    grad_self = jnp.pad(
        jnp.concatenate(in_order(pieces, member), axis=0), ((0, 0), (0, 256 - local))
    )
    second_grads = jnp.concatenate(
        [second_grads[:, h * 3 * hidden : (h + 1) * 3 * hidden] for h in range(head_count)], axis=0
    )
    grad_self = after(grad_self, second_grads)
    second_grads = lax.psum_scatter(second_grads, "head", scatter_dimension=0, tiled=True)
    second_grads = second_grads.astype(f32)
    grad_qkv = self_backward(qkv, grad_self, self_out, self_sums, starts)
    grad_normed = mm(grad_qkv, self_weights, NT)
    inverse = lax.rsqrt(jnp.mean(stream * stream, axis=-1, keepdims=True) + norm_eps)
    gain_one = jnp.sum(grad_normed * stream * inverse, axis=0)
    by_near = grad_normed.reshape(2, 2, row_count, width)
    kept = lax.dynamic_index_in_dim(by_near, core, 1, keepdims=False)
    came = lax.dynamic_index_in_dim(by_near, 1 - core, 1, keepdims=False).astype(bf16)
    self_core = mm(after(hidden_one, came), grad_qkv, TN).astype(bf16)
    kept = after(kept, self_core) + send(came, (1, 0)).astype(f32)
    came = send(pick(kept, 1 - near).astype(bf16), (0, 1))
    cross_chips = after(cross_chips, kept)
    cross_sums = chip_sum(cross_chips)
    memory_sum = after(memory_part[:, 0], cross_chips) + memory_came.astype(f32)
    memory_sum = memory_sum.astype(bf16)
    memory_sum = across(memory_sum)
    grad_normed = pick(kept, near) + came.astype(f32)
    grad_input, _ = rms_pull(stream_rows, gain_values[0], grad_normed)
    token_grads = (grad_rows + grad_input).astype(bf16)

    exit_self_part = mm(after(grad_low, token_grads), self_rows, TN).astype(bf16)
    kept, came = core_halves(exit_self_part)
    gain_part = jnp.stack([gain_one, gain_two, gain_three], axis=1).astype(bf16)
    gain_part = jnp.pad(gain_part, ((0, 0), (0, width - 3 * local - 3)))
    self_part = jnp.concatenate(
        [self_core[:, 256 * s : 256 * s + local] for s in range(3)] + [after(gain_part, token_grads)],
        axis=1,
    )
    self_part = self_part.reshape(chips, 2, shard, width)
    mine = lax.dynamic_index_in_dim(self_part, core, 1, keepdims=False)
    theirs = send(lax.dynamic_index_in_dim(self_part, 1 - core, 1, keepdims=False), (1, 0))
    token_grads = rows_within(token_grads)
    cross_sums = after(cross_sums, token_grads)
    token_grads = rows_across(token_grads)
    self_sums = jnp.stack(in_order([mine, theirs], core))
    self_sums = jnp.concatenate(
        [(kept.astype(f32) + came.astype(f32)).astype(bf16), self_sums], axis=0
    )
    self_sums = after(self_sums, cross_sums)
    token_grads = after(token_grads, self_sums, second_grads)
    self_sums = chip_sum(self_sums)

    sums = jnp.concatenate([self_sums[0:1], cross_sums, self_sums[1:3]], axis=0)
    sums = after(sums, token_grads, memory_sum)
    memory_grads = memory_sum.reshape(IMG_DEV, dp_count, patch_local, width).transpose(1, 0, 2, 3)
    memory_grads = lax.all_to_all(
        memory_grads.reshape(dp_count, IMG_DEV * patch_local, width),
        "dp",
        split_axis=0,
        concat_axis=0,
        tiled=True,
    )
    memory_grads = memory_grads.reshape(memory.shape).astype(f32)
    token_grads = rows_beside(token_grads).astype(f32)

    by_head = jnp.stack(
        [
            jnp.stack(
                [sums[w, :, h * local : (h + 1) * local] for w in range(3)]
                + [
                    sums[
                        3 + h // 2,
                        :,
                        w * half_width + (h % 2) * local : w * half_width + (h % 2 + 1) * local,
                    ]
                    for w in range(2)
                ]
                + [sums[5, :, 3 * local :] + sums[6, :, 3 * local :]]
            )
            for h in range(head_count)
        ]
    )
    by_head = by_head.reshape(2, 2, 6, shard, local)
    kept = lax.dynamic_index_in_dim(by_head, near, 1, keepdims=False)
    came = lax.dynamic_index_in_dim(by_head, 1 - near, 1, keepdims=False)
    kept = kept + send(came.astype(bf16), (0, 1)).astype(f32)
    self_grads = sums[5] + send(sums[6].astype(bf16), (0, 2)).astype(f32)
    first_grads = pick(kept, side) + send(pick(kept, 1 - side).astype(bf16), (0, 2)).astype(f32)
    exit_grads = jnp.stack([first_grads[0].T, first_grads[2].T])
    expand_grads = jnp.stack([second_grads[:, 0:hidden], second_grads[:, hidden : 2 * hidden]])
    contract_grads = second_grads[:, 2 * hidden :].T

    gain_grads = first_grads[5, :, 0:3].T
    entry_grads = jnp.stack(
        [self_grads[:, s * local : (s + 1) * local] for s in range(3)]
        + [first_grads[w] for w in (1, 3, 4)]
    )

    entry_mean, entry_square, entry_step = lamb_step(
        entry_weights, entry_grads, entry_first, entry_second, weight_decay
    )
    exit_mean, exit_square, exit_step = lamb_step(
        exit_weights, exit_grads, exit_first, exit_second, weight_decay
    )
    expand_mean, expand_square, expand_step = lamb_step(
        expand_weights, expand_grads, expand_first, expand_second, weight_decay
    )
    contract_mean, contract_square, contract_step = lamb_step(
        contract_weights, contract_grads, contract_first, contract_second, weight_decay
    )
    gains_mean, gains_square, gains_step = lamb_step(
        norm_gains, gain_grads, gains_first, gains_second, 0.0
    )
    weight_local = jnp.concatenate(
        [
            jnp.sum(entry_weights * entry_weights, axis=(1, 2)),
            jnp.sum(exit_weights * exit_weights, axis=(1, 2)),
            jnp.sum(expand_weights * expand_weights, axis=(1, 2)),
            jnp.sum(contract_weights * contract_weights).reshape(1),
            jnp.sum(norm_gains * norm_gains, axis=1) / head_count,
        ]
    )
    step_local = jnp.concatenate(
        [
            jnp.sum(entry_step * entry_step, axis=(1, 2)),
            jnp.sum(exit_step * exit_step, axis=(1, 2)),
            jnp.sum(expand_step * expand_step, axis=(1, 2)),
            jnp.sum(contract_step * contract_step).reshape(1),
            jnp.sum(gains_step * gains_step, axis=1) / head_count,
        ]
    )
    weight_squares, step_squares = all_sum(after(jnp.stack([weight_local, step_local]), token_grads, memory_grads))
    weight_norm = jnp.sqrt(weight_squares)
    step_norm = jnp.sqrt(step_squares)
    ratio = learn_rate * weight_norm / (step_norm + adam_eps)
    entry_new = entry_weights - ratio[0:6][:, None, None] * entry_step
    exit_new = exit_weights - ratio[6:8][:, None, None] * exit_step
    expand_new = expand_weights - ratio[8:10][:, None, None] * expand_step
    contract_new = contract_weights - ratio[10] * contract_step
    gains_new = norm_gains - ratio[11:14][:, None] * gains_step
    trust_norms = jnp.stack([weight_norm, step_norm])
    return (
        output,
        token_grads,
        memory_grads,
        entry_grads,
        exit_grads,
        expand_grads,
        contract_grads,
        gain_grads,
        entry_mean,
        exit_mean,
        expand_mean,
        contract_mean,
        gains_mean,
        entry_square,
        exit_square,
        expand_square,
        contract_square,
        gains_square,
        entry_new,
        exit_new,
        expand_new,
        contract_new,
        gains_new,
        entry_new.astype(jnp.bfloat16),
        exit_new.astype(jnp.bfloat16),
        expand_new.astype(jnp.bfloat16),
        contract_new.astype(jnp.bfloat16),
        trust_norms,
    )


def solution(mesh):
    in_specs = (
        P("dp", None),
        P(None, ("dp", "head"), None),
        P("dp", None),
        P("dp"),
        P("dp"),
        P("dp"),
        P(None, "dp", "head"),
        P(None, "head", "dp"),
        P(None, "dp", "head"),
        P("head", "dp"),
        P(None, "dp"),
        P(None, "dp", "head"),
        P(None, "dp", "head"),
        P(None, "head", "dp"),
        P(None, "head", "dp"),
        P(None, "dp", "head"),
        P(None, "dp", "head"),
        P("head", "dp"),
        P("head", "dp"),
        P(None, "dp"),
        P(None, "dp"),
    )
    out_specs = (
        P("dp", None),
        P("dp", None),
        P(None, ("dp", "head"), None),
        P(None, "dp", "head"),
        P(None, "head", "dp"),
        P(None, "dp", "head"),
        P("head", "dp"),
        P(None, "dp"),
        P(None, "dp", "head"),
        P(None, "head", "dp"),
        P(None, "dp", "head"),
        P("head", "dp"),
        P(None, "dp"),
        P(None, "dp", "head"),
        P(None, "head", "dp"),
        P(None, "dp", "head"),
        P("head", "dp"),
        P(None, "dp"),
        P(None, "dp", "head"),
        P(None, "head", "dp"),
        P(None, "dp", "head"),
        P("head", "dp"),
        P(None, "dp"),
        P(None, "dp", "head"),
        P(None, "head", "dp"),
        P(None, "dp", "head"),
        P("head", "dp"),
        P(),
    )
    return jax.shard_map(
        per_device, mesh=mesh, in_specs=in_specs, out_specs=out_specs, check_vma=False
    )
```
